256 devices in a mesh: dp: 16 (over z, x_hi), mp: 16 (over y, x_lo, core).
Axes of the slice: x: 4 (x_hi: 2, x_lo: 2; x = x_hi * 2 + x_lo), y: 4, z: 8, core: 2. Of those that a mesh axis runs over, the one named last changes fastest.
Arguments:
- inputs: bfloat16 [4096, 4096], P('dp', 'mp'), may hold values from -50 to 50
- cotangent: bfloat16 [4096, 4096], P('dp', 'mp'), may hold values from -50 to 50
- w_up: bfloat16 [4096, 16384], P('dp', 'mp'), may hold values from -0.09375 to 0.09375
- w_down: bfloat16 [16384, 4096], P('mp', 'dp'), may hold values from -0.046875 to 0.046875
Outputs:
- input_grad: bfloat16 [4096, 4096], P('dp', 'mp')
- up_grad: float32 [4096, 16384], P('dp', 'mp')
- down_grad: float32 [16384, 4096], P('mp', 'dp')
- mean_square: float32 [], replicated
The draws below stay inside these ranges and needn't reach their ends.
All inputs are finite; a program needn't handle non-finite values.
Results may differ from the reference program's by a relative error of at most 0.018.
Values may be sent and summed in bfloat16 or wider, within the bound.
A program may use at most 128 MiB of HBM per device.

```python
import jax
import jax.numpy as jnp
from jax import lax

D = 4096
FF = 16384
TOK_DEV = 256
TOKENS = 4096
N_DP = 16


def shape_field(key, base, top):
    pairing = jax.random.permutation(jax.random.fold_in(key, 11), N_DP)
    rows = jnp.arange(TOKENS, dtype=jnp.int32) // TOK_DEV
    cols = jnp.arange(D, dtype=jnp.int32) // (D // N_DP)
    paired = pairing[rows][:, None] == cols[None, :]
    spike = jnp.where(paired, jnp.float32(2.5), jnp.float32(1.0))
    column_scale = jnp.float32(top) ** (jnp.arange(D, dtype=jnp.float32) / jnp.float32(D - 1))
    return base * column_scale[None, :] * spike


def draw_inputs(key, part):
    key = jax.random.fold_in(key, 1)
    base = jax.random.truncated_normal(key, -4.0, 4.0, (TOKENS, D), jnp.float32)
    top = 3.0
    return shape_field(key, base, top).astype(jnp.bfloat16)


def draw_cotangent(key, part):
    key = jax.random.fold_in(key, 2)
    base = jax.random.truncated_normal(key, -4.0, 4.0, (TOKENS, D), jnp.float32)
    top = 3.0
    return shape_field(key, base, top).astype(jnp.bfloat16)


def level_of(rng, extent, split, low, high):
    def one(dim, parts):
        steps = jax.random.uniform(jax.random.fold_in(jax.random.fold_in(rng, 6), dim), (parts,), jnp.float32, low / len(split), high / len(split))
        return jnp.repeat(jnp.exp(steps), extent[dim] // parts).reshape((-1,) + (1,) * (len(extent) - dim - 1))

    level = one(*split[0])
    for cut in split[1:]:
        level = level * one(*cut)
    return level


def bell_draw(stream_key, shape, scale, limit, split=(), kind=jnp.bfloat16):
    result = jax.random.normal(stream_key, shape, jnp.float32) * scale
    if len(split) > 0:
        result = level_of(stream_key, shape, split, -0.22, 0.18) * result
    return jnp.clip(result, min=-limit, max=limit).astype(kind)


def setup_inputs(seed: int = 0) -> dict:
    key_of = jax.random.split(jax.random.key(seed), 5)
    return {
        "inputs": draw_inputs(jax.random.fold_in(key_of[4], 71), 0),
        "cotangent": draw_cotangent(jax.random.fold_in(key_of[4], 71), 0),
        "w_up": bell_draw(key_of[2], (D, FF), D ** -0.5, 0.09375, ((0, 16), (1, 16))),
        "w_down": bell_draw(key_of[3], (FF, D), FF ** -0.5, 0.046875, ((0, 16), (1, 16))),
    }


root_half = 0.7071067811865476
inv_root_two_pi = 0.3989422804014327

def gelu_value(hidden):
    return 0.5 * hidden * (1.0 + jax.scipy.special.erf(hidden * root_half))

def gelu_slope(hidden):
    return 0.5 * (1.0 + jax.scipy.special.erf(hidden * root_half)) + hidden * jnp.exp(-0.5 * hidden * hidden) * inv_root_two_pi

def block_sum(left, right):
    left_blocks = left.reshape(N_DP, TOK_DEV, left.shape[1])
    right_blocks = right.reshape(N_DP, TOK_DEV, right.shape[1])

    def step(total, pair):
        term = lax.dot_general(pair[0], pair[1], (((0,), (0,)), ((), ())), preferred_element_type=jnp.float32)
        rounded = lax.optimization_barrier(term.astype(jnp.bfloat16)).astype(jnp.float32)
        return (total + rounded, None)
    start = jnp.zeros((left.shape[1], right.shape[1]), jnp.float32)
    total, unused = lax.scan(step, start, (left_blocks, right_blocks))
    return total

def reference(inputs, cotangent, w_up, w_down):
    hidden = jnp.dot(inputs, w_up, preferred_element_type=jnp.float32)
    act = gelu_value(hidden).astype(jnp.bfloat16)
    grad_act = lax.dot_general(cotangent, w_down, (((1,), (1,)), ((), ())), preferred_element_type=jnp.float32)
    grad_pre = (grad_act * gelu_slope(hidden)).astype(jnp.bfloat16)
    input_grad = lax.dot_general(grad_pre, w_up, (((1,), (1,)), ((), ())), preferred_element_type=jnp.float32).astype(jnp.bfloat16)
    raw_up = block_sum(inputs, grad_pre)
    raw_down = block_sum(act, cotangent)
    total_sq = jnp.sum(raw_up * raw_up) + jnp.sum(raw_down * raw_down)
    mean_square = total_sq / jnp.float32(2.0 * D * FF)
    scale = 1.0 / jnp.sqrt(mean_square)
    return (input_grad, raw_up * scale, raw_down * scale, mean_square)
```

```python
import jax
import jax.numpy as jnp
from jax import lax
from jax.experimental import pallas as pl
from jax.experimental.pallas import tpu as pltpu
from jax.sharding import PartitionSpec as P

D = 4096
FF = 16384

NX, NY, NZ = 4, 4, 8
XT = 64
TZ = 2 * XT
TOK = NZ * TZ
KB = 256
UB = 128
UN = 2 * UB
ROW = NZ * KB
CUT = 768
NQ = 2
QR = UB // NQ

MESH = pl.DeviceIdType.MESH
BF = jnp.bfloat16
F32 = jnp.float32

root_half = 0.7071067811865476
inv_root_two_pi = 0.3989422804014327


def step(value, offset, size):
    return lax.rem(value + (offset + size), size)


def span(start, size):
    return pl.ds(pl.multiple_of(start, size), size)


def dot_nt(left, right):
    return lax.dot_general(
        left, right, (((1,), (1,)), ((), ())), preferred_element_type=F32
    )


def dot_nn(left, right):
    return lax.dot_general(
        left, right, (((1,), (0,)), ((), ())), preferred_element_type=F32
    )


def kernel(
    xy_in, w_in, ig_out, grad_out, sq_out,
    xy, ww, hid, gact, act_t, pre, pre_t,
    part, r1r, r1l, r2r, r2l, red, land,
    ig_send, ig_recv, py, y1r, y1l, y2r, y2l, ty, zl, fz, ox, nb,
    send, recv, local,
):
    dp, mp = lax.axis_index("dp"), lax.axis_index("mp")
    z, xh = lax.div(dp, 2), lax.rem(dp, 2)
    y, xl, c = lax.div(mp, 4), lax.rem(lax.div(mp, 2), 2), lax.rem(mp, 2)
    x = 2 * xh + xl

    def device(px, py_, pz, pc):
        return (pz * 2 + lax.div(px, 2), py_ * 4 + lax.rem(px, 2) * 2 + pc)

    def at_x(k):
        return device(step(x, k, NX), y, z, c)

    def at_y(k):
        return device(x, step(y, k, NY), z, c)

    def at_z(k):
        return device(x, y, step(z, k, NZ), c)

    sibling = device(x, y, z, 1 - c)

    started = []

    def push(src, dst, target):
        n = len(started)
        copy = pltpu.make_async_remote_copy(
            src_ref=src, dst_ref=dst, send_sem=send.at[n], recv_sem=recv.at[n],
            device_id=target, device_id_type=MESH,
        )
        copy.start()
        started.append(copy)
        return copy

    def land_all(copies):
        for copy in copies:
            copy.wait_recv()

    barrier = pltpu.get_barrier_semaphore()
    peers = (
        [at_x(k) for k in range(1, NX)]
        + [at_y(k) for k in range(1, NY)]
        + [at_z(k) for k in range(1, NZ)]
        + [sibling]
    )
    for peer in peers:
        pl.semaphore_signal(barrier, inc=1, device_id=peer, device_id_type=MESH)
    pl.semaphore_wait(barrier, len(peers))

    first, rest = pl.ds(0, CUT), pl.ds(CUT, 4 * KB - CUT)

    def rows(pz):
        return span(pz * TZ, TZ)

    def half(pz, which):
        return span(pz * TZ + which * XT, XT)

    def cols(pz):
        return span(pz * KB, KB)

    tok_place = xy.at[c, y, span(z * TZ + xh * XT, XT), span(xl * 2 * KB, 2 * KB)]
    tok_own = pltpu.make_async_copy(xy_in.at[span(x * XT, XT), :], tok_place, local.at[0])
    tok_own.start()
    tok = []
    for k in (1, 3, 2):
        px = step(x, k, NX)
        tok.append(push(xy_in.at[span(px * XT, XT), :], tok_place, at_x(k)))

    w_place = ww.at[x, :, :, cols(z)]
    w_own = pltpu.make_async_copy(w_in.at[:, span(z * UB, UB), :], w_place, local.at[1])
    w_own.start()
    wz = {}

    def w_send(k):
        pz = step(z, k, NZ)
        wz[k] = push(w_in.at[:, span(pz * UB, UB), :], w_place, at_z(k))

    for k in (1, 7, 2, 6):
        w_send(k)

    wx1, wx2 = {}, {}

    def w_hop1(k):
        piece = ww.at[x, :, :, cols(step(z, -k, NZ))]
        wx1[k] = [push(piece, piece, at_x(1)), push(piece, piece, at_x(-1))]

    def w_hop2(k):
        land_all(wx1[k])
        pz = cols(step(z, -k, NZ))
        right = ww.at[step(x, -1, NX), 0, :, pz]
        left = ww.at[step(x, 1, NX), 1, :, pz]
        wx2[k] = [push(right, right, at_x(1)), push(left, left, at_x(-1))]

    ya1, ya2, ca, cb, za, zb = {}, {}, {}, {}, {}, {}

    def ya_hop1(k):
        block = xy.at[c, y, rows(step(z, k, NZ)), first]
        ya1[k] = [push(block, block, at_y(1)), push(block, block, at_y(-1))]

    def ya_hop2(k):
        land_all(ya1[k])
        pz = step(z, k, NZ)
        right = xy.at[c, step(y, -1, NY), half(pz, 0), first]
        left = xy.at[c, step(y, 1, NY), half(pz, 1), first]
        ya2[k] = [push(right, right, at_y(1)), push(left, left, at_y(-1))]

    def ya_core(k):
        land_all(ya2[k])
        block = xy.at[c, :, rows(step(z, k, NZ)), first]
        ca[k] = push(block, block, sibling)

    def za_step(k):
        if k < 4:
            right = xy.at[c, y, rows(step(z, 1 - k, NZ)), first]
            left = xy.at[c, y, rows(step(z, k - 1, NZ)), first]
        else:
            right = xy.at[c, y, half(step(z, 1 - k, NZ), 0), first]
            left = xy.at[c, y, half(step(z, k - 1, NZ), 1), first]
        za[k] = [push(right, right, at_z(1)), push(left, left, at_z(-1))]

    def zb_step(k):
        if k < 4:
            right = xy.at[c, :, rows(step(z, 1 - k, NZ)), rest]
            left = xy.at[c, :, rows(step(z, k - 1, NZ)), rest]
        else:
            right = xy.at[c, :, half(step(z, 1 - k, NZ), 0), rest]
            left = xy.at[c, :, half(step(z, k - 1, NZ), 1), rest]
        zb[k] = [push(right, right, at_z(1)), push(left, left, at_z(-1))]

    def cb_core(k):
        block = xy.at[c, :, rows(step(z, k, NZ)), rest]
        cb[k] = push(block, block, sibling)

    tok_own.wait()
    land_all(tok)
    block = xy.at[c, y, rows(z), rest]
    yb1 = [push(block, block, at_y(1)), push(block, block, at_y(-1))]
    za_step(1)
    ya_hop1(0)
    w_own.wait()
    w_hop1(0)

    land_all(yb1)
    right = xy.at[c, step(y, -1, NY), half(z, 0), rest]
    left = xy.at[c, step(y, 1, NY), half(z, 1), rest]
    yb2 = [push(right, right, at_y(1)), push(left, left, at_y(-1))]
    land_all(za[1])
    za_step(2)
    ya_hop1(1)
    ya_hop1(-1)

    land_all(yb2)
    zb_step(1)
    cb_core(0)
    for k in (3, 5, 4):
        w_send(k)
    for k in (1, 7):
        wz[k].wait_recv()
        w_hop1(k)
    ya_hop2(0)

    land_all(za[2])
    za_step(3)
    ya_hop1(2)
    ya_hop1(-2)
    w_hop2(0)

    land_all(zb[1])
    zb_step(2)
    cb_core(1)
    cb_core(-1)
    for k in (2, 6):
        wz[k].wait_recv()
        w_hop1(k)
    ya_hop2(1)
    ya_hop2(-1)

    land_all(za[3])
    za_step(4)
    ya_hop1(3)
    ya_hop1(-3)
    w_hop2(1)
    w_hop2(7)
    ya_core(0)

    land_all(zb[2])
    zb_step(3)
    cb_core(2)
    cb_core(-2)
    for k in (3, 5):
        wz[k].wait_recv()
        w_hop1(k)
    ya_hop2(2)
    ya_hop2(-2)

    land_all(za[4])
    ya_hop1(4)
    w_hop2(2)
    w_hop2(6)
    ya_core(1)
    ya_core(-1)

    land_all(zb[3])
    zb_step(4)
    cb_core(3)
    cb_core(-3)
    wz[4].wait_recv()
    w_hop1(4)
    w_hop2(3)
    w_hop2(5)
    ya_hop2(3)
    ya_hop2(-3)
    w_hop2(4)
    ya_core(2)
    ya_core(-2)
    ya_hop2(4)
    land_all(zb[4])
    cb_core(4)
    ya_core(3)
    ya_core(-3)
    ya_core(4)
    for k in range(NZ):
        land_all(wx2[k])
    for k in ca:
        ca[k].wait_recv()
        cb[k].wait_recv()

    hid[...] = jnp.zeros_like(hid)
    gact[...] = jnp.zeros_like(gact)

    def weight(which, pc, start, size):
        return ww[pl.ds(2 * pc, 2), which, :, span(start, size)].reshape(UN, size)

    def operand(which, p):
        return xy[
            lax.div(p, NZ), lax.div(lax.rem(p, NZ), 2), :,
            span((2 * lax.rem(p, 2) + which) * KB, KB),
        ]

    @pl.loop(0, 16)
    def _(p):
        pc, start = lax.div(p, NZ), lax.rem(p, NZ) * KB
        hid[...] += dot_nt(operand(0, p), weight(0, pc, start, KB))
        gact[...] += dot_nt(operand(1, p), weight(1, pc, start, KB))

    @pl.loop(0, NZ)
    def _(t):
        at = span(t * TZ, TZ)
        h = hid[at, :]
        both = 0.5 * (1.0 + lax.erf(h * root_half))
        act = (h * both).astype(BF)
        slope = both + h * jnp.exp(-0.5 * h * h) * inv_root_two_pi
        grad = (gact[at, :] * slope).astype(BF)
        pre[at, :] = grad
        pre_t[:, at] = grad.T
        act_t[:, at] = act.T

    def ig_part(pc, py_, h, at):
        return dot_nn(pre[at, :], weight(0, pc, (2 * py_ + h) * KB, KB))

    igc = {}
    for k in (2, 1, -1, 0):
        py_ = step(y, k, NY)
        for h in range(2):
            @pl.loop(0, 4)
            def _(t):
                at = span(t * 256, 256)
                ig_send[py_, h, at, :] = ig_part(1 - c, py_, h, at).astype(BF)

            igc[k, h] = push(ig_send.at[py_, h], ig_recv.at[py_, h], sibling)

    def grad_parts(pc):
        @pl.loop(0, NZ)
        def _(q):
            p = pc * NZ + q
            for a, left in ((0, pre_t), (1, act_t)):
                out = dot_nn(left[...], operand(a, p)).astype(BF)
                part[2 * pc, a, :, cols(q)] = out[:UB]
                part[2 * pc + 1, a, :, cols(q)] = out[UB:]

    grad_parts(1 - xh)
    x1 = {}
    for q in range(NQ):
        at = pl.ds(q * QR, QR)
        far = step(x, 2, NX)
        x1[q] = [
            push(part.at[far, 0, at, :], r1r.at[q], at_x(1)),
            push(part.at[far, 1, at, :], r1l.at[q], at_x(-1)),
        ]

    def ig_own(py_, h, at):
        return ig_part(c, py_, h, at) + ig_recv[py_, h, at, :].astype(F32)

    y1 = {}
    for h in range(2):
        py_ = step(y, 2, NY)
        igc[2, h].wait_recv()

        @pl.loop(0, 4)
        def _(t):
            at = span(t * 256, 256)
            py[0, h, at, :] = ig_own(py_, h, at).astype(BF)

        y1[h] = [
            push(py.at[0, h, pl.ds(0, TOK // 2), :], y1r.at[h], at_y(1)),
            push(py.at[0, h, pl.ds(TOK // 2, TOK // 2), :], y1l.at[h], at_y(-1)),
        ]

    grad_parts(xh)

    x2 = {}
    for q in range(NQ):
        at = pl.ds(q * QR, QR)
        land_all(x1[q])
        nxt, prv = step(x, 1, NX), step(x, -1, NX)
        for px, a, got in ((nxt, 0, r1r), (prv, 1, r1l)):
            total = part[px, a, at, :].astype(F32) + got[q].astype(F32)
            part[px, a, at, :] = total.astype(BF)
        x2[q] = [
            push(part.at[nxt, :, at, :], r2r.at[q], at_x(1)),
            push(part.at[prv, :, at, :], r2l.at[q], at_x(-1)),
        ]

    y2 = {}
    for h in range(2):
        land_all(y1[h])
        for k, slot, mine, got in ((1, 1, 0, y1r), (-1, 2, 1, y1l)):
            py_ = step(y, k, NY)
            igc[k, h].wait_recv()
            for side in range(2):
                @pl.loop(0, 2)
                def _(t):
                    at = span(side * (TOK // 2) + t * 256, 256)
                    total = ig_own(py_, h, at)
                    if side == mine:
                        total = total + got[h, span(t * 256, 256), :].astype(F32)
                    py[slot, h, at, :] = total.astype(BF)

        y2[h] = [
            push(py.at[1, h], y2r.at[h], at_y(1)),
            push(py.at[2, h], y2l.at[h], at_y(-1)),
        ]

    gz, gz_own = [], []
    for q in range(NQ):
        at = pl.ds(q * QR, QR)
        land_all(x2[q])
        for a in range(2):
            total = (
                part[x, a, at, :].astype(F32)
                + r2r[q, a].astype(F32)
                + r2l[q, a].astype(F32)
            )
            red[q, a] = total.astype(BF)
        place = land.at[:, span(z * UB + q * QR, QR), :]
        own = pltpu.make_async_copy(red.at[q, :, :, cols(z)], place, local.at[2 + q])
        own.start()
        gz_own.append(own)
        for k in (1, 7, 2, 6, 3, 5, 4):
            gz.append(push(red.at[q, :, :, cols(step(z, k, NZ))], place, at_z(k)))

    iz = {}
    for h in range(2):
        land_all(y2[h])
        igc[0, h].wait_recv()

        @pl.loop(0, 4)
        def _(t):
            at = span(t * 256, 256)
            total = ig_own(y, h, at) + y2r[h, at, :].astype(F32) + y2l[h, at, :].astype(F32)
            ty[h, at, :] = total.astype(BF)

        zl[h, z] = ty[h, rows(z), :]
        iz[h] = [
            push(ty.at[h, rows(step(z, k, NZ)), :], zl.at[h, z], at_z(k))
            for k in (1, 7, 2, 6, 3, 5, 4)
        ]

    for copy in gz_own:
        copy.wait()
    land_all(gz)

    def square(t, total):
        for a in range(2):
            v = land[a, span(t * 64, 64), :].astype(F32)
            total = total + jnp.sum(v * v, axis=0, keepdims=True)
        return total

    squares = lax.fori_loop(0, 16, square, jnp.zeros((1, KB), F32))
    value = jnp.sum(squares, axis=1, keepdims=True)

    def exchange(stage, me, size, targets, value):
        nb[stage, me] = jnp.broadcast_to(value, (8, 128))
        return [push(nb.at[stage, me], nb.at[stage, me], t) for t in targets]

    def collect(stage, size, copies):
        land_all(copies)
        total = nb[stage, 0]
        for n in range(1, size):
            total = total + nb[stage, n]
        return total[:1, :1]

    norm = exchange(0, z, NZ, [at_z(k) for k in range(1, NZ)], value)

    for h in range(2):
        land_all(iz[h])
        total = zl[h, 0].astype(F32)
        for n in range(1, NZ):
            total = total + zl[h, n].astype(F32)
        fz[h] = total.astype(BF)

    def last(px):
        return fz.at[lax.rem(px, 2), span(lax.div(px, 2) * XT, XT), :]

    o_place = ox.at[span(x * XT, XT), :]
    o_own = pltpu.make_async_copy(last(x), o_place, local.at[2 + NQ])
    o_own.start()
    o_far = [push(last(step(x, k, NX)), o_place, at_x(k)) for k in (1, 3, 2)]

    value = collect(0, NZ, norm)
    norm = exchange(1, x, NX, [at_x(k) for k in range(1, NX)], value)
    grad_out[...] = land[...]
    value = collect(1, NX, norm)
    norm = exchange(2, y, NY, [at_y(k) for k in range(1, NY)], value)
    o_own.wait()
    land_all(o_far)
    ig_out[...] = ox[...]
    value = collect(2, NY, norm)
    norm = exchange(3, c, 2, [sibling], value)
    value = collect(3, 2, norm)
    sq_out[...] = jnp.broadcast_to(value, (8, 128))

    for copy in started:
        copy.wait_send()


def on_device(inputs, cotangent, w_up, w_down):
    xy = jnp.concatenate([inputs, cotangent], axis=1)
    w = jnp.stack([w_up.T, w_down])
    vmem = pl.BlockSpec(memory_space=pltpu.VMEM)
    hbm = pl.BlockSpec(memory_space=pl.ANY)
    ig, grads, total = pl.pallas_call(
        kernel,
        out_shape=(
            jax.ShapeDtypeStruct((NX * XT, KB), BF),
            jax.ShapeDtypeStruct((2, NZ * UB, KB), BF),
            jax.ShapeDtypeStruct((8, 128), F32),
        ),
        in_specs=[hbm, hbm],
        out_specs=(vmem, vmem, vmem),
        scratch_shapes=[
            pltpu.VMEM((2, NY, TOK, 4 * KB), BF),
            pltpu.VMEM((NX, 2, UB, ROW), BF),
            pltpu.VMEM((TOK, UN), F32),
            pltpu.VMEM((TOK, UN), F32),
            pltpu.VMEM((UN, TOK), BF),
            pltpu.VMEM((TOK, UN), BF),
            pltpu.VMEM((UN, TOK), BF),
            pltpu.VMEM((NX, 2, UB, ROW), BF),
            pltpu.VMEM((NQ, QR, ROW), BF),
            pltpu.VMEM((NQ, QR, ROW), BF),
            pltpu.VMEM((NQ, 2, QR, ROW), BF),
            pltpu.VMEM((NQ, 2, QR, ROW), BF),
            pltpu.VMEM((NQ, 2, QR, ROW), BF),
            pltpu.VMEM((2, NZ * UB, KB), BF),
            pltpu.VMEM((NY, 2, TOK, KB), BF),
            pltpu.VMEM((NY, 2, TOK, KB), BF),
            pltpu.VMEM((3, 2, TOK, KB), BF),
            pltpu.VMEM((2, TOK // 2, KB), BF),
            pltpu.VMEM((2, TOK // 2, KB), BF),
            pltpu.VMEM((2, TOK, KB), BF),
            pltpu.VMEM((2, TOK, KB), BF),
            pltpu.VMEM((2, TOK, KB), BF),
            pltpu.VMEM((2, NZ, TZ, KB), BF),
            pltpu.VMEM((2, TZ, KB), BF),
            pltpu.VMEM((NX * XT, KB), BF),
            pltpu.VMEM((4, NZ, 8, 128), F32),
            pltpu.SemaphoreType.DMA((200,)),
            pltpu.SemaphoreType.DMA((200,)),
            pltpu.SemaphoreType.DMA((8,)),
        ],
        compiler_params=pltpu.CompilerParams(
            collective_id=0, has_side_effects=True, vmem_limit_bytes=60 * 2**20
        ),
        cost_estimate=pl.CostEstimate(
            flops=11_000_000_000, bytes_accessed=8_000_000, transcendentals=524288
        ),
    )(xy, w)
    mean_square = total[0, 0] / jnp.float32(2.0 * D * FF)
    scale = 1.0 / jnp.sqrt(mean_square)
    up = grads[0].T.astype(F32) * scale
    down = grads[1].astype(F32) * scale
    return ig, up, down, mean_square


def solution(mesh):
    placed = (P("dp", "mp"), P("dp", "mp"), P("dp", "mp"), P("mp", "dp"))
    return jax.shard_map(
        on_device,
        mesh=mesh,
        in_specs=placed,
        out_specs=(P("dp", "mp"), P("dp", "mp"), P("mp", "dp"), P()),
        check_vma=False,
    )
```

```python
import jax
import jax.numpy as jnp
from jax import lax
from jax.experimental import pallas as pl
from jax.experimental.pallas import tpu as pltpu
from jax.sharding import PartitionSpec as P

D = 4096
FF = 16384

NX, NY, NZ = 4, 4, 8
XT = 64
TZ = 2 * XT
TOK = NZ * TZ
KB = 256
UB = 128
UN = 2 * UB
ROW = NZ * KB
CUT = 768
NQ = 4
QR = UB // NQ

MESH = pl.DeviceIdType.MESH
BF = jnp.bfloat16
F32 = jnp.float32

root_half = 0.7071067811865476
inv_root_two_pi = 0.3989422804014327


def step(value, offset, size):
    return lax.rem(value + (offset + size), size)


def span(start, size):
    return pl.ds(pl.multiple_of(start, size), size)


def dot_nt(left, right):
    return lax.dot_general(
        left, right, (((1,), (1,)), ((), ())), preferred_element_type=F32
    )


def dot_nn(left, right):
    return lax.dot_general(
        left, right, (((1,), (0,)), ((), ())), preferred_element_type=F32
    )


def kernel(
    x_in, dy_in, wu_in, wd_in, ig_out, up_out, down_out, sq_out,
    wu, ws, xy, ww, wt, wsib, hid, gact, act_t, pre, pre_t, pre_sib,
    part, r1r, r1l, r2r, r2l, red, land,
    py, y1r, y1l, y2r, y2l, ty, z_r, z_l, fz, ox, nb,
    send, recv, local,
):
    dp, mp = lax.axis_index("dp"), lax.axis_index("mp")
    z, xh = lax.div(dp, 2), lax.rem(dp, 2)
    y, xl, c = lax.div(mp, 4), lax.rem(lax.div(mp, 2), 2), lax.rem(mp, 2)
    x = 2 * xh + xl

    def device(px, py_, pz, pc):
        return (pz * 2 + lax.div(px, 2), py_ * 4 + lax.rem(px, 2) * 2 + pc)

    def at_x(k):
        return device(step(x, k, NX), y, z, c)

    def at_y(k):
        return device(x, step(y, k, NY), z, c)

    def at_z(k):
        return device(x, y, step(z, k, NZ), c)

    sibling = device(x, y, z, 1 - c)

    started = []

    def push(src, dst, target):
        n = len(started)
        copy = pltpu.make_async_remote_copy(
            src_ref=src, dst_ref=dst, send_sem=send.at[n], recv_sem=recv.at[n],
            device_id=target, device_id_type=MESH,
        )
        copy.start()
        started.append(copy)
        return copy

    moved = []

    def move(src, dst):
        copy = pltpu.make_async_copy(src, dst, local.at[len(moved)])
        copy.start()
        moved.append(copy)
        return copy

    def land_all(copies):
        for copy in copies:
            copy.wait_recv()

    wu_own = move(wu_in, wu)
    wd_own = move(wd_in, ws.at[1])

    barrier = pltpu.get_barrier_semaphore()
    plane = [
        device(step(x, i, NX), step(y, j, NY), z, c)
        for i in range(NX) for j in range(NY) if i or j
    ]
    column = [
        device(x, y, step(z, k, NZ), pc)
        for k in range(NZ) for pc in (c, 1 - c) if k or pc is not c
    ]
    peers = plane + column
    for peer in peers:
        pl.semaphore_signal(barrier, inc=1, device_id=peer, device_id_type=MESH)

    wu_own.wait()

    @pl.loop(0, NZ)
    def _(t):
        at = span(t * UB, UB)
        ws[0, at, :] = wu[:, at].T

    wd_own.wait()
    pl.semaphore_wait(barrier, len(peers))

    first, rest = pl.ds(0, CUT), pl.ds(CUT, 4 * KB - CUT)

    def rows(pz):
        return span(pz * TZ, TZ)

    def half(pz, which):
        return span(pz * TZ + which * XT, XT)

    def cols(pz):
        return span(pz * KB, KB)

    def tok_place(a):
        return xy.at[c, y, span(z * TZ + xh * XT, XT), span((xl * 2 + a) * KB, KB)]

    tok, tok_own = [], []
    for k in (1, 3, 2):
        px = step(x, k, NX)
        for a, source in ((0, x_in), (1, dy_in)):
            tok.append(push(source.at[span(px * XT, XT), :], tok_place(a), at_x(k)))
    for a, source in ((0, x_in), (1, dy_in)):
        tok_own.append(move(source.at[span(x * XT, XT), :], tok_place(a)))

    w_place = ww.at[x, :, :, cols(z)]
    wz = {}

    def w_send(k):
        wz[k] = push(ws.at[:, span(step(z, k, NZ) * UB, UB), :], w_place, at_z(k))

    for k in (1, 7, 2, 6):
        w_send(k)
    w_own = move(ws.at[:, span(z * UB, UB), :], w_place)

    wx1, wx2 = {}, {}

    def w_hop1(k):
        if k:
            wz[k].wait_recv()
        piece = ww.at[x, :, :, cols(step(z, -k, NZ))]
        wx1[k] = [push(piece, piece, at_x(1)), push(piece, piece, at_x(-1))]

    def w_hop2(k):
        land_all(wx1[k])
        pz = cols(step(z, -k, NZ))
        right = ww.at[step(x, -1, NX), 0, :, pz]
        left = ww.at[step(x, 1, NX), 1, :, pz]
        wx2[k] = [push(right, right, at_x(1)), push(left, left, at_x(-1))]

    ya1, ya2, ca, cb, za, zb = {}, {}, {}, {}, {}, {}

    def ya_hop1(k):
        block = xy.at[c, y, rows(step(z, k, NZ)), first]
        ya1[k] = [push(block, block, at_y(1)), push(block, block, at_y(-1))]

    def ya_hop2(k):
        land_all(ya1[k])
        pz = step(z, k, NZ)
        right = xy.at[c, step(y, -1, NY), half(pz, 0), first]
        left = xy.at[c, step(y, 1, NY), half(pz, 1), first]
        ya2[k] = [push(right, right, at_y(1)), push(left, left, at_y(-1))]

    def ya_core(k):
        land_all(ya2[k])
        block = xy.at[c, :, rows(step(z, k, NZ)), first]
        ca[k] = push(block, block, sibling)

    def za_step(k):
        if k < 4:
            right = xy.at[c, y, rows(step(z, 1 - k, NZ)), first]
            left = xy.at[c, y, rows(step(z, k - 1, NZ)), first]
        else:
            right = xy.at[c, y, half(step(z, 1 - k, NZ), 0), first]
            left = xy.at[c, y, half(step(z, k - 1, NZ), 1), first]
        za[k] = [push(right, right, at_z(1)), push(left, left, at_z(-1))]

    def zb_step(k):
        if k < 4:
            right = xy.at[c, :, rows(step(z, 1 - k, NZ)), rest]
            left = xy.at[c, :, rows(step(z, k - 1, NZ)), rest]
        else:
            right = xy.at[c, :, half(step(z, 1 - k, NZ), 0), rest]
            left = xy.at[c, :, half(step(z, k - 1, NZ), 1), rest]
        zb[k] = [push(right, right, at_z(1)), push(left, left, at_z(-1))]

    def cb_core(k):
        block = xy.at[c, :, rows(step(z, k, NZ)), rest]
        cb[k] = push(block, block, sibling)

    def weight(which, pc, start):
        return ww[pl.ds(2 * pc, 2), which, :, span(start, KB)].reshape(UN, KB)

    def turn(k):
        land_all(wx2[k])
        pz = step(z, -k, NZ)

        @pl.loop(0, 2)
        def _(pc):
            for a in range(2):
                wt[a, pc, pz] = weight(a, pc, pz * KB).T

    pre_far = {}

    def hidden(ks):
        for k in ks:
            ca[k].wait_recv()
            cb[k].wait_recv()
        places = [rows(step(z, k, NZ)) for k in ks]
        size = TZ * len(ks)

        def operand(a, p):
            got = [
                jnp.concatenate(
                    [
                        xy[lax.div(p, NY), lax.rem(p, NY), at, pl.ds((2 * n + a) * KB, KB)]
                        for n in range(2)
                    ],
                    axis=1,
                )
                for at in places
            ]
            return got[0] if len(got) == 1 else jnp.concatenate(got, axis=0)

        hid[:size] = jnp.zeros((size, UN), F32)
        gact[:size] = jnp.zeros((size, UN), F32)

        @pl.loop(0, 2 * NY)
        def _(p):
            pair = pl.ds(2 * lax.rem(p, NY), 2)
            for a, total in ((0, hid), (1, gact)):
                right = wt[a, lax.div(p, NY), pair].reshape(2 * KB, UN)
                total[:size] += dot_nn(operand(a, p), right)

        for n, (k, at) in enumerate(zip(ks, places)):
            h = hid[n * TZ : (n + 1) * TZ]
            both = 0.5 * (1.0 + lax.erf(h * root_half))
            act = (h * both).astype(BF)
            slope = both + h * jnp.exp(-0.5 * h * h) * inv_root_two_pi
            grad = (gact[n * TZ : (n + 1) * TZ] * slope).astype(BF)
            pre[at, :] = grad
            pre_t[:, at] = grad.T
            act_t[:, at] = act.T
            pre_far[k] = push(pre.at[at, :], pre_sib.at[at, :], sibling)

    for copy in tok_own:
        copy.wait()
    land_all(tok)
    block = xy.at[c, y, rows(z), rest]
    yb1 = [push(block, block, at_y(1)), push(block, block, at_y(-1))]
    za_step(1)
    ya_hop1(0)
    w_own.wait()
    w_hop1(0)
    w_hop1(1)
    w_hop1(7)

    land_all(yb1)
    right = xy.at[c, step(y, -1, NY), half(z, 0), rest]
    left = xy.at[c, step(y, 1, NY), half(z, 1), rest]
    yb2 = [push(right, right, at_y(1)), push(left, left, at_y(-1))]
    w_hop1(2)
    w_hop1(6)
    land_all(yb2)
    zb_step(1)
    cb_core(0)
    ya_hop2(0)
    land_all(za[1])
    za_step(2)
    ya_hop1(1)
    ya_hop1(-1)
    w_hop2(0)
    w_hop2(1)
    w_hop2(7)
    ya_core(0)
    land_all(zb[1])
    zb_step(2)
    cb_core(1)
    cb_core(-1)
    w_hop2(2)
    w_hop2(6)
    land_all(za[2])
    za_step(3)
    w_send(3)
    w_send(5)
    w_send(4)
    ya_hop1(2)
    ya_hop1(-2)
    ya_hop2(1)
    ya_hop2(-1)
    for k in (0, 1, 7):
        turn(k)
    land_all(zb[2])
    cb_core(2)
    cb_core(-2)
    ya_core(1)
    ya_core(-1)
    land_all(za[3])
    za_step(4)
    zb_step(3)
    ya_hop1(3)
    ya_hop1(-3)
    turn(2)
    turn(6)
    ya_hop2(2)
    ya_hop2(-2)
    w_hop1(3)
    w_hop1(5)
    ya_core(2)
    ya_core(-2)
    w_hop1(4)
    land_all(za[4])
    ya_hop1(4)
    w_hop2(3)
    w_hop2(5)
    ya_hop2(3)
    ya_hop2(-3)
    w_hop2(4)
    land_all(zb[3])
    zb_step(4)
    cb_core(3)
    cb_core(-3)
    ya_core(3)
    ya_core(-3)
    for k in (3, 5, 4):
        turn(k)
    w_far = push(ww.at[pl.ds(2 * (1 - c), 2), 0, :, :], wsib, sibling)
    hidden((1, -1))
    ya_hop2(4)
    hidden((2, -2))
    land_all(zb[4])
    cb_core(4)
    ya_core(4)
    hidden((0, 3))
    hidden((-3, 4))

    def grad_parts(pc, a):
        left = pre_t if a == 0 else act_t

        @pl.loop(0, NZ)
        def _(q):
            right = xy[
                pc, lax.div(q, 2), :, span((2 * lax.rem(q, 2) + a) * KB, KB)
            ]
            out = dot_nn(left[...], right).astype(BF)
            part[2 * pc, a, :, cols(q)] = out[:UB]
            part[2 * pc + 1, a, :, cols(q)] = out[UB:]

    far, nxt, prv = step(x, 2, NX), step(x, 1, NX), step(x, -1, NX)
    x1, x2, gz, gz_own = {}, {}, [], []

    def piece(q):
        return pl.ds(q * QR, QR)

    def x_step1(q, a):
        src = part.at[far, a, piece(q), :]
        if a == 0:
            x1[q] = [push(src, r1r.at[q], at_x(1))]
        else:
            x1[q].append(push(src, r1l.at[q], at_x(-1)))

    def x_step2(q):
        land_all(x1[q])
        for px, a, got in ((nxt, 0, r1r), (prv, 1, r1l)):
            total = part[px, a, piece(q), :].astype(F32) + got[q].astype(F32)
            part[px, a, piece(q), :] = total.astype(BF)
        x2[q] = [
            push(part.at[nxt, :, piece(q), :], r2r.at[q], at_x(1)),
            push(part.at[prv, :, piece(q), :], r2l.at[q], at_x(-1)),
        ]

    def x_step3(q):
        land_all(x2[q])
        for a in range(2):
            total = (
                part[x, a, piece(q), :].astype(F32)
                + r2r[q, a].astype(F32)
                + r2l[q, a].astype(F32)
            )
            red[q, a] = total.astype(BF)
        place = land.at[:, span(z * UB + q * QR, QR), :]
        for k in (1, 7, 2, 6, 3, 5, 4):
            gz.append(push(red.at[q, :, :, cols(step(z, k, NZ))], place, at_z(k)))
        gz_own.append(move(red.at[q, :, :, cols(z)], place))

    half_tok = TOK // 2

    def ig_own(py_, h, side):
        at = pl.ds(side * half_tok, half_tok)
        start = (2 * py_ + h) * KB
        near = weight(0, c, start)
        other = wsib[:, :, span(start, KB)].reshape(UN, KB)
        return dot_nn(pre[at, :], near) + dot_nn(pre_sib[at, :], other)

    y1, y2 = {}, {}

    def y_step1(h):
        for side in range(2):
            at = pl.ds(side * half_tok, half_tok)
            py[0, h, at, :] = ig_own(step(y, 2, NY), h, side).astype(BF)
        y1[h] = [
            push(py.at[0, h, pl.ds(0, half_tok), :], y1r.at[h], at_y(1)),
            push(py.at[0, h, pl.ds(half_tok, half_tok), :], y1l.at[h], at_y(-1)),
        ]

    def y_step2(h):
        for k, slot, mine, got in ((1, 1, 0, y1r), (-1, 2, 1, y1l)):
            for side in range(2):
                at = pl.ds(side * half_tok, half_tok)
                total = ig_own(step(y, k, NY), h, side)
                if side == mine:
                    y1[h][mine].wait_recv()
                    total = total + got[h].astype(F32)
                py[slot, h, at, :] = total.astype(BF)
        y2[h] = [
            push(py.at[1, h], y2r.at[h], at_y(1)),
            push(py.at[2, h], y2l.at[h], at_y(-1)),
        ]

    def y_step3(h):
        land_all(y2[h])
        for side in range(2):
            at = pl.ds(side * half_tok, half_tok)
            total = (
                ig_own(y, h, side)
                + y2r[h, at, :].astype(F32)
                + y2l[h, at, :].astype(F32)
            )
            ty[h, at, :] = total.astype(BF)

    iz = {}

    def z_step(h, k):
        right, left = step(z, 5 - k, NZ), step(z, k - 5, NZ)
        if k == 1:
            iz[h, 1] = [
                push(ty.at[h, half(right, 0), :], z_r.at[h, 0, pl.ds(0, XT), :], at_z(1)),
                push(ty.at[h, half(left, 1), :], z_l.at[h, 0, pl.ds(XT, XT), :], at_z(-1)),
            ]
            return
        land_all(iz[h, k - 1])
        if k == 2:
            add_r, add_l = half(right, 0), half(left, 1)
            got_r, got_l = z_r[h, 0, :XT], z_l[h, 0, XT:]
        else:
            add_r, add_l = rows(right), rows(left)
            got_r, got_l = z_r[h, k - 2], z_l[h, k - 2]
        for at, got in ((add_r, got_r), (add_l, got_l)):
            ty[h, at, :] = (ty[h, at, :].astype(F32) + got.astype(F32)).astype(BF)
        iz[h, k] = [
            push(ty.at[h, rows(right), :], z_r.at[h, k - 1], at_z(1)),
            push(ty.at[h, rows(left), :], z_l.at[h, k - 1], at_z(-1)),
        ]

    def z_last(h):
        land_all(iz[h, 4])
        total = (
            ty[h, rows(z), :].astype(F32)
            + z_r[h, 3].astype(F32)
            + z_l[h, 3].astype(F32)
        )
        fz[h] = total.astype(BF)

    grad_parts(1 - xh, 0)
    x_step1(0, 0)
    x_step1(1, 0)
    for k in pre_far:
        pre_far[k].wait_recv()
    w_far.wait_recv()
    y_step1(0)
    grad_parts(1 - xh, 1)
    x_step1(0, 1)
    x_step1(1, 1)
    y_step1(1)
    grad_parts(xh, 0)
    grad_parts(xh, 1)
    x_step2(0)
    x_step1(2, 0)
    x_step1(2, 1)
    y_step2(0)
    x_step2(1)
    x_step1(3, 0)
    x_step1(3, 1)
    y_step2(1)
    x_step3(0)
    x_step2(2)
    x_step3(1)
    y_step3(0)
    z_step(0, 1)
    x_step2(3)
    z_step(0, 2)
    x_step3(2)
    z_step(0, 3)
    z_step(0, 4)
    y_step3(1)
    z_step(1, 1)
    x_step3(3)
    z_last(0)
    z_step(1, 2)
    z_step(1, 3)

    for copy in gz_own:
        copy.wait()
    land_all(gz)

    def square(t, total):
        for a in range(2):
            v = land[a, span(t * 64, 64), :].astype(F32)
            total = total + jnp.sum(v * v, axis=0, keepdims=True)
        return total

    squares = lax.fori_loop(0, 16, square, jnp.zeros((1, KB), F32))
    value = jnp.sum(squares, axis=1, keepdims=True)

    def exchange(stage, me, targets, value):
        nb[stage, me] = jnp.broadcast_to(value, (8, 128))
        return [push(nb.at[stage, me], nb.at[stage, me], t) for t in targets]

    def collect(stage, copies):
        land_all(copies)
        total = nb[stage, 0]
        for n in range(1, 16):
            total = total + nb[stage, n]
        return total[:1, :1]

    norm = exchange(0, 2 * z + c, column, value)
    z_step(1, 4)
    down_out[...] = land[1]
    value = collect(0, norm)
    norm = exchange(1, 4 * x + y, plane, value)
    z_last(1)

    def last(px):
        return fz.at[lax.rem(px, 2), span(lax.div(px, 2) * XT, XT), :]

    o_place = ox.at[span(x * XT, XT), :]
    o_far = [push(last(step(x, k, NX)), o_place, at_x(k)) for k in (1, 3, 2)]
    o_own = move(last(x), o_place)

    @pl.loop(0, NZ)
    def _(t):
        at = span(t * UB, UB)
        up_out[:, at] = land[0, at, :].T

    value = collect(1, norm)
    sq_out[...] = jnp.broadcast_to(value, (8, 128))
    o_own.wait()
    land_all(o_far)
    ig_out[...] = ox[...]

    for copy in started:
        copy.wait_send()


def on_device(inputs, cotangent, w_up, w_down):
    vmem = pl.BlockSpec(memory_space=pltpu.VMEM)
    hbm = pl.BlockSpec(memory_space=pl.ANY)
    ig, up, down, total = pl.pallas_call(
        kernel,
        out_shape=(
            jax.ShapeDtypeStruct((NX * XT, KB), BF),
            jax.ShapeDtypeStruct((KB, NZ * UB), BF),
            jax.ShapeDtypeStruct((NZ * UB, KB), BF),
            jax.ShapeDtypeStruct((8, 128), F32),
        ),
        in_specs=[hbm] * 4,
        out_specs=(vmem,) * 4,
        scratch_shapes=[
            pltpu.VMEM((KB, NZ * UB), BF),
            pltpu.VMEM((2, NZ * UB, KB), BF),
            pltpu.VMEM((2, NY, TOK, 4 * KB), BF),
            pltpu.VMEM((NX, 2, UB, ROW), BF),
            pltpu.VMEM((2, 2, NZ, KB, UN), BF),
            pltpu.VMEM((2, UB, ROW), BF),
            pltpu.VMEM((2 * TZ, UN), F32),
            pltpu.VMEM((2 * TZ, UN), F32),
            pltpu.VMEM((UN, TOK), BF),
            pltpu.VMEM((TOK, UN), BF),
            pltpu.VMEM((UN, TOK), BF),
            pltpu.VMEM((TOK, UN), BF),
            pltpu.VMEM((NX, 2, UB, ROW), BF),
            pltpu.VMEM((NQ, QR, ROW), BF),
            pltpu.VMEM((NQ, QR, ROW), BF),
            pltpu.VMEM((NQ, 2, QR, ROW), BF),
            pltpu.VMEM((NQ, 2, QR, ROW), BF),
            pltpu.VMEM((NQ, 2, QR, ROW), BF),
            pltpu.VMEM((2, NZ * UB, KB), BF),
            pltpu.VMEM((3, 2, TOK, KB), BF),
            pltpu.VMEM((2, TOK // 2, KB), BF),
            pltpu.VMEM((2, TOK // 2, KB), BF),
            pltpu.VMEM((2, TOK, KB), BF),
            pltpu.VMEM((2, TOK, KB), BF),
            pltpu.VMEM((2, TOK, KB), BF),
            pltpu.VMEM((2, 4, TZ, KB), BF),
            pltpu.VMEM((2, 4, TZ, KB), BF),
            pltpu.VMEM((2, TZ, KB), BF),
            pltpu.VMEM((NX * XT, KB), BF),
            pltpu.VMEM((2, 16, 8, 128), F32),
            pltpu.SemaphoreType.DMA((240,)),
            pltpu.SemaphoreType.DMA((240,)),
            pltpu.SemaphoreType.DMA((16,)),
        ],
        compiler_params=pltpu.CompilerParams(
            collective_id=0, has_side_effects=True, vmem_limit_bytes=60 * 2**20
        ),
        cost_estimate=pl.CostEstimate(
            flops=11_000_000_000, bytes_accessed=8_000_000, transcendentals=524288
        ),
    )(inputs, cotangent, w_up, w_down)
    mean_square = total[0, 0] / jnp.float32(2.0 * D * FF)
    scale = 1.0 / jnp.sqrt(mean_square)
    return ig, up.astype(F32) * scale, down.astype(F32) * scale, mean_square


def solution(mesh):
    placed = (P("dp", "mp"), P("dp", "mp"), P("dp", "mp"), P("mp", "dp"))
    return jax.shard_map(
        on_device,
        mesh=mesh,
        in_specs=placed,
        out_specs=(P("dp", "mp"), P("dp", "mp"), P("mp", "dp"), P()),
        check_vma=False,
    )
```

```python
import jax
import jax.numpy as jnp
from jax import lax
from jax.experimental import pallas as pl
from jax.experimental.pallas import tpu as pltpu
from jax.sharding import PartitionSpec as P

D = 4096
FF = 16384

NX, NY, NZ = 4, 4, 8
XT = 64
TZ = 2 * XT
TOK = NZ * TZ
KB = 256
UB = 128
UN = 2 * UB
ROW = NZ * KB
CUT = 768
PIECES = (0, 16, 32, 64, 96, 112, 128)

MESH = pl.DeviceIdType.MESH
BF = jnp.bfloat16
F32 = jnp.float32

root_half = 0.7071067811865476
inv_root_two_pi = 0.3989422804014327


def step(value, offset, size):
    return lax.rem(value + (offset + size), size)


def span(start, size):
    return pl.ds(pl.multiple_of(start, size), size)


def dot_nt(left, right):
    return lax.dot_general(
        left, right, (((1,), (1,)), ((), ())), preferred_element_type=F32
    )


def dot_nn(left, right):
    return lax.dot_general(
        left, right, (((1,), (0,)), ((), ())), preferred_element_type=F32
    )


def kernel(
    x_in, dy_in, wu_in, wd_in, ig_out, up_out, down_out, sq_out,
    wu, ws, xy, ww, wt, wsib, hid, gact, act_t, pre, pre_t, pre_sib,
    part, r1r, r1l, r2r, r2l, red, land,
    py, y1r, y1l, y2r, y2l, ty, z_r, z_l, fz, ox, nb,
    send, recv, local,
):
    dp, mp = lax.axis_index("dp"), lax.axis_index("mp")
    z, xh = lax.div(dp, 2), lax.rem(dp, 2)
    y, xl, c = lax.div(mp, 4), lax.rem(lax.div(mp, 2), 2), lax.rem(mp, 2)
    x = 2 * xh + xl

    def device(px, py_, pz, pc):
        return (pz * 2 + lax.div(px, 2), py_ * 4 + lax.rem(px, 2) * 2 + pc)

    def at_x(k):
        return device(step(x, k, NX), y, z, c)

    def at_y(k):
        return device(x, step(y, k, NY), z, c)

    def at_z(k):
        return device(x, y, step(z, k, NZ), c)

    sibling = device(x, y, z, 1 - c)

    started = []

    def push(src, dst, target):
        n = len(started)
        copy = pltpu.make_async_remote_copy(
            src_ref=src, dst_ref=dst, send_sem=send.at[n], recv_sem=recv.at[n],
            device_id=target, device_id_type=MESH,
        )
        copy.start()
        started.append(copy)
        return copy

    moved = []

    def move(src, dst):
        copy = pltpu.make_async_copy(src, dst, local.at[len(moved)])
        copy.start()
        moved.append(copy)
        return copy

    def land_all(copies):
        for copy in copies:
            copy.wait_recv()

    wu_own = move(wu_in, wu)
    wd_own = move(wd_in, ws.at[1])

    barrier = pltpu.get_barrier_semaphore()
    plane = [
        device(step(x, i, NX), step(y, j, NY), z, c)
        for i in range(NX) for j in range(NY) if i or j
    ]
    column = [
        device(x, y, step(z, k, NZ), pc)
        for k in range(NZ) for pc in (c, 1 - c) if k or pc is not c
    ]
    peers = plane + column
    for peer in peers:
        pl.semaphore_signal(barrier, inc=1, device_id=peer, device_id_type=MESH)

    pl.semaphore_wait(barrier, len(peers))

    first, rest = pl.ds(0, CUT), pl.ds(CUT, 4 * KB - CUT)

    def rows(pz):
        return span(pz * TZ, TZ)

    def half(pz, which):
        return span(pz * TZ + which * XT, XT)

    def cols(pz):
        return span(pz * KB, KB)

    def tok_place(a):
        return xy.at[c, y, span(z * TZ + xh * XT, XT), span((xl * 2 + a) * KB, KB)]

    tok, tok_own = [], []
    for k in (1, 3, 2):
        px = step(x, k, NX)
        for a, source in ((0, x_in), (1, dy_in)):
            tok.append(push(source.at[span(px * XT, XT), :], tok_place(a), at_x(k)))
    for a, source in ((0, x_in), (1, dy_in)):
        tok_own.append(move(source.at[span(x * XT, XT), :], tok_place(a)))

    wu_own.wait()

    @pl.loop(0, NZ)
    def _(t):
        at = span(t * UB, UB)
        ws[0, at, :] = wu[:, at].T

    wd_own.wait()
    w_place = ww.at[x, :, :, cols(z)]
    wz = {}

    def w_send(k):
        wz[k] = push(ws.at[:, span(step(z, k, NZ) * UB, UB), :], w_place, at_z(k))

    w_send(1)
    w_send(7)
    w_own = move(ws.at[:, span(z * UB, UB), :], w_place)

    wx1, wx2 = {}, {}

    direct = (3, 5, 4)

    def w_hop1(k):
        if k:
            wz[k].wait_recv()
        piece = ww.at[x, :, :, cols(step(z, -k, NZ))]
        wx1[k] = [push(piece, piece, at_x(1)), push(piece, piece, at_x(-1))]
        if k in direct:
            wx2[k] = [push(piece, piece, at_x(2))]

    def w_hop2(k):
        land_all(wx1[k])
        if k in direct:
            return
        pz = cols(step(z, -k, NZ))
        right = ww.at[step(x, -1, NX), 0, :, pz]
        left = ww.at[step(x, 1, NX), 1, :, pz]
        wx2[k] = [push(right, right, at_x(1)), push(left, left, at_x(-1))]

    ya1, ya2, ca, cb, za, zb = {}, {}, {}, {}, {}, {}

    def ya_hop1(k):
        block = xy.at[c, y, rows(step(z, k, NZ)), first]
        ya1[k] = [push(block, block, at_y(1)), push(block, block, at_y(-1))]

    def ya_hop2(k):
        land_all(ya1[k])
        pz = step(z, k, NZ)
        right = xy.at[c, step(y, -1, NY), half(pz, 0), first]
        left = xy.at[c, step(y, 1, NY), half(pz, 1), first]
        ya2[k] = [push(right, right, at_y(1)), push(left, left, at_y(-1))]

    def ya_core(k):
        land_all(ya2[k])
        block = xy.at[c, :, rows(step(z, k, NZ)), first]
        ca[k] = push(block, block, sibling)

    def za_step(k):
        if k < 4:
            right = xy.at[c, y, rows(step(z, 1 - k, NZ)), first]
            left = xy.at[c, y, rows(step(z, k - 1, NZ)), first]
        else:
            right = xy.at[c, y, half(step(z, 1 - k, NZ), 0), first]
            left = xy.at[c, y, half(step(z, k - 1, NZ), 1), first]
        za[k] = [push(right, right, at_z(1)), push(left, left, at_z(-1))]

    def zb_step(k):
        if k < 4:
            right = xy.at[c, :, rows(step(z, 1 - k, NZ)), rest]
            left = xy.at[c, :, rows(step(z, k - 1, NZ)), rest]
        else:
            right = xy.at[c, :, half(step(z, 1 - k, NZ), 0), rest]
            left = xy.at[c, :, half(step(z, k - 1, NZ), 1), rest]
        zb[k] = [push(right, right, at_z(1)), push(left, left, at_z(-1))]

    def cb_core(k):
        block = xy.at[c, :, rows(step(z, k, NZ)), rest]
        cb[k] = push(block, block, sibling)

    def weight(which, pc, start):
        return ww[pl.ds(2 * pc, 2), which, :, span(start, KB)].reshape(UN, KB)

    def turn(k):
        land_all(wx2[k])
        pz = step(z, -k, NZ)

        @pl.loop(0, 2)
        def _(pc):
            for a in range(2):
                wt[a, pc, pz] = weight(a, pc, pz * KB).T

    pre_far = {}

    def hidden(ks):
        for k in ks:
            ca[k].wait_recv()
            cb[k].wait_recv()
        places = [rows(step(z, k, NZ)) for k in ks]
        size = TZ * len(ks)

        def operand(a, p):
            got = [
                jnp.concatenate(
                    [
                        xy[lax.div(p, NY), lax.rem(p, NY), at, pl.ds((2 * n + a) * KB, KB)]
                        for n in range(2)
                    ],
                    axis=1,
                )
                for at in places
            ]
            return got[0] if len(got) == 1 else jnp.concatenate(got, axis=0)

        hid[:size] = jnp.zeros((size, UN), F32)
        gact[:size] = jnp.zeros((size, UN), F32)

        @pl.loop(0, 2 * NY)
        def _(p):
            pair = pl.ds(2 * lax.rem(p, NY), 2)
            for a, total in ((0, hid), (1, gact)):
                right = wt[a, lax.div(p, NY), pair].reshape(2 * KB, UN)
                total[:size] += dot_nn(operand(a, p), right)

        for n, (k, at) in enumerate(zip(ks, places)):
            pz = step(z, k, NZ)
            h = hid[n * TZ : (n + 1) * TZ]
            both = 0.5 * (1.0 + lax.erf(h * root_half))
            act = (h * both).astype(BF)
            slope = both + h * jnp.exp(-0.5 * h * h) * inv_root_two_pi
            grad = (gact[n * TZ : (n + 1) * TZ] * slope).astype(BF)
            pre[pz] = grad
            pre_t[:, at] = grad.T
            act_t[:, at] = act.T
            pre_far[k] = push(pre.at[pz], pre_sib.at[pz], sibling)

    for copy in tok_own:
        copy.wait()
    land_all(tok)
    block = xy.at[c, y, rows(z), rest]
    yb1 = [push(block, block, at_y(1)), push(block, block, at_y(-1))]
    za_step(1)
    ya_hop1(0)
    w_send(2)
    w_send(6)
    w_own.wait()
    w_hop1(0)
    w_hop1(1)
    w_hop1(7)

    land_all(yb1)
    right = xy.at[c, step(y, -1, NY), half(z, 0), rest]
    left = xy.at[c, step(y, 1, NY), half(z, 1), rest]
    yb2 = [push(right, right, at_y(1)), push(left, left, at_y(-1))]
    land_all(za[1])
    za_step(2)
    ya_hop1(1)
    ya_hop1(-1)
    ya_hop2(0)
    land_all(yb2)
    zb_step(1)
    cb_core(0)
    w_hop1(2)
    w_hop1(6)
    w_hop2(0)
    w_hop2(1)
    w_hop2(7)
    land_all(za[2])
    za_step(3)
    ya_hop1(2)
    ya_hop1(-2)
    w_send(3)
    w_send(5)
    ya_hop2(1)
    ya_hop2(-1)
    ya_core(0)
    land_all(zb[1])
    zb_step(2)
    cb_core(1)
    cb_core(-1)
    w_hop2(2)
    w_hop2(6)
    turn(0)
    turn(1)
    turn(7)
    land_all(za[3])
    za_step(4)
    w_send(4)
    ya_hop1(3)
    ya_hop1(-3)
    turn(2)
    turn(6)
    ya_hop2(2)
    ya_hop2(-2)
    ya_core(1)
    ya_core(-1)
    w_hop1(3)
    w_hop1(5)
    land_all(zb[2])
    zb_step(3)
    cb_core(2)
    cb_core(-2)
    land_all(za[4])
    ya_hop1(4)
    ya_hop2(3)
    ya_hop2(-3)
    ya_core(2)
    ya_core(-2)
    w_hop2(3)
    w_hop2(5)
    turn(3)
    turn(5)
    w_hop1(4)
    land_all(zb[3])
    zb_step(4)
    cb_core(3)
    cb_core(-3)
    ya_hop2(4)
    ya_core(3)
    ya_core(-3)
    w_hop2(4)
    turn(4)
    w_far = push(ww.at[pl.ds(2 * (1 - c), 2), 0, :, :], wsib, sibling)
    ya_core(4)
    hidden((0, 1, -1, 2, -2))
    land_all(zb[4])
    cb_core(4)
    hidden((3, -3, 4))

    def grad_parts(pc, a):
        left = pre_t if a == 0 else act_t

        @pl.loop(0, NZ)
        def _(q):
            right = xy[
                pc, lax.div(q, 2), :, span((2 * lax.rem(q, 2) + a) * KB, KB)
            ]
            out = dot_nn(left[...], right).astype(BF)
            part[2 * pc, a, :, cols(q)] = out[:UB]
            part[2 * pc + 1, a, :, cols(q)] = out[UB:]

    far, nxt, prv = step(x, 2, NX), step(x, 1, NX), step(x, -1, NX)
    x1, x2, gz, gz_own = {}, {}, {}, {}

    def piece(q):
        return pl.ds(PIECES[q], PIECES[q + 1] - PIECES[q])

    def x_step1(q, a):
        src = part.at[far, a, piece(q), :]
        if a == 0:
            x1[q] = [push(src, r1r.at[piece(q), :], at_x(1))]
        else:
            x1[q].append(push(src, r1l.at[piece(q), :], at_x(-1)))

    def x_step2(q):
        land_all(x1[q])
        at = piece(q)
        for px, a, got in ((nxt, 0, r1r), (prv, 1, r1l)):
            total = part[px, a, at, :].astype(F32) + got[at, :].astype(F32)
            part[px, a, at, :] = total.astype(BF)
        x2[q] = [
            push(part.at[nxt, :, at, :], r2r.at[:, at, :], at_x(1)),
            push(part.at[prv, :, at, :], r2l.at[:, at, :], at_x(-1)),
        ]

    def x_step3(q):
        land_all(x2[q])
        at = piece(q)
        for a in range(2):
            total = (
                part[x, a, at, :].astype(F32)
                + r2r[a, at, :].astype(F32)
                + r2l[a, at, :].astype(F32)
            )
            red[a, at, :] = total.astype(BF)
        place = land.at[:, pl.ds(pl.multiple_of(z * UB + PIECES[q], 16), at.size), :]
        gz[q] = [
            push(red.at[:, at, cols(step(z, k, NZ))], place, at_z(k))
            for k in (1, 7, 2, 6, 3, 5, 4)
        ]
        gz_own[q] = move(red.at[:, at, cols(z)], place)

    def squares(q, total):
        gz_own[q].wait()
        land_all(gz[q])
        at = piece(q)
        for a in range(2):
            for n in range(NZ):
                v = land[a, pl.ds(n * UB + at.start, at.size), :].astype(F32)
                total = total + jnp.sum(v * v, axis=0, keepdims=True)
        return total

    pieces = (2, 1, 3, 0)
    size = NZ * XT

    def ig_own(py_, j):
        px = step(x, pieces[j], NX)
        tokens = span(lax.div(px, 2) * XT, XT)
        start = (2 * py_ + lax.rem(px, 2)) * KB
        near = weight(0, c, start)
        other = wsib[:, :, span(start, KB)].reshape(UN, KB)
        return dot_nn(pre[:, tokens, :].reshape(size, UN), near) + dot_nn(
            pre_sib[:, tokens, :].reshape(size, UN), other
        )

    y1, y2 = {}, {}
    low, high = pl.ds(0, size // 2), pl.ds(size // 2, size // 2)

    def y_step1(j):
        py[0, j] = ig_own(step(y, 2, NY), j).astype(BF)
        y1[j] = [
            push(py.at[0, j, low, :], y1r.at[j], at_y(1)),
            push(py.at[0, j, high, :], y1l.at[j], at_y(-1)),
        ]

    def y_step2(j):
        total = ig_own(step(y, 1, NY), j)
        y1[j][0].wait_recv()
        py[1, j, low, :] = (total[: size // 2] + y1r[j].astype(F32)).astype(BF)
        py[1, j, high, :] = total[size // 2 :].astype(BF)
        right = push(py.at[1, j], y2r.at[j], at_y(1))
        total = ig_own(step(y, -1, NY), j)
        y1[j][1].wait_recv()
        py[2, j, low, :] = total[: size // 2].astype(BF)
        py[2, j, high, :] = (total[size // 2 :] + y1l[j].astype(F32)).astype(BF)
        y2[j] = [right, push(py.at[2, j], y2l.at[j], at_y(-1))]

    def y_step3(j):
        total = ig_own(y, j)
        land_all(y2[j])
        ty[j] = (total + y2r[j].astype(F32) + y2l[j].astype(F32)).astype(BF)

    iz = {}
    XH = XT // 2

    def band(pz):
        return span(pz * XT, XT)

    def part_band(pz, which):
        return span(pz * XT + which * XH, XH)

    def z_step(j, k):
        right, left = step(z, 5 - k, NZ), step(z, k - 5, NZ)
        if k == 1:
            iz[j, 1] = [
                push(ty.at[j, part_band(right, 0), :], z_r.at[j, 0, pl.ds(0, XH), :], at_z(1)),
                push(ty.at[j, part_band(left, 1), :], z_l.at[j, 0, pl.ds(XH, XH), :], at_z(-1)),
            ]
            return
        land_all(iz[j, k - 1])
        if k == 2:
            add_r, add_l = part_band(right, 0), part_band(left, 1)
            got_r, got_l = z_r[j, 0, :XH], z_l[j, 0, XH:]
        else:
            add_r, add_l = band(right), band(left)
            got_r, got_l = z_r[j, k - 2], z_l[j, k - 2]
        for at, got in ((add_r, got_r), (add_l, got_l)):
            ty[j, at, :] = (ty[j, at, :].astype(F32) + got.astype(F32)).astype(BF)
        iz[j, k] = [
            push(ty.at[j, band(right), :], z_r.at[j, k - 1], at_z(1)),
            push(ty.at[j, band(left), :], z_l.at[j, k - 1], at_z(-1)),
        ]

    far_out = []

    def z_last(j):
        land_all(iz[j, 4])
        total = (
            ty[j, band(z), :].astype(F32)
            + z_r[j, 3].astype(F32)
            + z_l[j, 3].astype(F32)
        ).astype(BF)
        if pieces[j]:
            fz[j] = total
            far_out.append(
                push(fz.at[j], ox.at[span(x * XT, XT), :], at_x(pieces[j]))
            )
        else:
            ox[span(x * XT, XT), :] = total

    grad_parts(1 - xh, 0)
    for q in range(4):
        x_step1(q, 0)
    for k in pre_far:
        pre_far[k].wait_recv()
    w_far.wait_recv()
    y_step1(0)
    y_step1(1)
    grad_parts(1 - xh, 1)
    for q in range(4):
        x_step1(q, 1)
    y_step1(2)
    grad_parts(xh, 0)
    grad_parts(xh, 1)
    x_step2(0)
    y_step2(0)
    x_step2(1)
    y_step1(3)
    y_step2(1)
    x_step2(2)
    for q in (4, 5):
        x_step1(q, 0)
        x_step1(q, 1)
    x_step3(0)
    y_step2(2)
    x_step3(1)
    y_step3(0)
    x_step2(3)
    y_step2(3)
    x_step3(2)
    y_step3(1)
    z_step(0, 1)
    z_step(1, 1)
    x_step2(4)
    x_step2(5)
    y_step3(2)
    z_step(0, 2)
    z_step(1, 2)
    x_step3(3)
    total = squares(0, jnp.zeros((1, KB), F32))
    total = squares(1, total)
    y_step3(3)
    z_step(2, 1)
    z_step(3, 1)
    z_step(0, 3)
    z_step(1, 3)
    x_step3(4)
    x_step3(5)
    total = squares(2, total)
    z_step(2, 2)
    z_step(3, 2)
    z_step(0, 4)
    z_step(1, 4)
    total = squares(3, total)
    z_step(2, 3)
    z_step(3, 3)
    total = squares(4, total)

    total = squares(5, total)
    value = jnp.sum(total, axis=1, keepdims=True)

    def exchange(stage, me, targets, value):
        nb[stage, me] = jnp.broadcast_to(value, (8, 128))
        return [push(nb.at[stage, me], nb.at[stage, me], t) for t in targets]

    def collect(stage, copies):
        land_all(copies)
        total = nb[stage, 0]
        for n in range(1, 16):
            total = total + nb[stage, n]
        return total[:1, :1]

    norm = exchange(0, 2 * z + c, column, value)
    z_last(0)
    z_last(1)
    z_step(2, 4)
    z_step(3, 4)
    value = collect(0, norm)
    norm = exchange(1, 4 * x + y, plane, value)
    down_out[...] = land[1]
    z_last(2)

    @pl.loop(0, NZ)
    def _(t):
        at = span(t * UB, UB)
        up_out[:, at] = land[0, at, :].T

    z_last(3)
    land_all(far_out)
    ig_out[...] = ox[...]
    value = collect(1, norm)
    sq_out[0, 0] = jnp.max(value)

    for copy in started:
        copy.wait_send()


def on_device(inputs, cotangent, w_up, w_down):
    vmem = pl.BlockSpec(memory_space=pltpu.VMEM)
    hbm = pl.BlockSpec(memory_space=pl.ANY)
    ig, up, down, total = pl.pallas_call(
        kernel,
        out_shape=(
            jax.ShapeDtypeStruct((NX * XT, KB), BF),
            jax.ShapeDtypeStruct((KB, NZ * UB), BF),
            jax.ShapeDtypeStruct((NZ * UB, KB), BF),
            jax.ShapeDtypeStruct((1, 1), F32),
        ),
        in_specs=[hbm] * 4,
        out_specs=(vmem, vmem, vmem, pl.BlockSpec(memory_space=pltpu.SMEM)),
        scratch_shapes=[
            pltpu.VMEM((KB, NZ * UB), BF),
            pltpu.VMEM((2, NZ * UB, KB), BF),
            pltpu.VMEM((2, NY, TOK, 4 * KB), BF),
            pltpu.VMEM((NX, 2, UB, ROW), BF),
            pltpu.VMEM((2, 2, NZ, KB, UN), BF),
            pltpu.VMEM((2, UB, ROW), BF),
            pltpu.VMEM((5 * TZ, UN), F32),
            pltpu.VMEM((5 * TZ, UN), F32),
            pltpu.VMEM((UN, TOK), BF),
            pltpu.VMEM((NZ, TZ, UN), BF),
            pltpu.VMEM((UN, TOK), BF),
            pltpu.VMEM((NZ, TZ, UN), BF),
            pltpu.VMEM((NX, 2, UB, ROW), BF),
            pltpu.VMEM((UB, ROW), BF),
            pltpu.VMEM((UB, ROW), BF),
            pltpu.VMEM((2, UB, ROW), BF),
            pltpu.VMEM((2, UB, ROW), BF),
            pltpu.VMEM((2, UB, ROW), BF),
            pltpu.VMEM((2, NZ * UB, KB), BF),
            pltpu.VMEM((3, 4, NZ * XT, KB), BF),
            pltpu.VMEM((4, NZ * XT // 2, KB), BF),
            pltpu.VMEM((4, NZ * XT // 2, KB), BF),
            pltpu.VMEM((4, NZ * XT, KB), BF),
            pltpu.VMEM((4, NZ * XT, KB), BF),
            pltpu.VMEM((4, NZ * XT, KB), BF),
            pltpu.VMEM((4, 4, XT, KB), BF),
            pltpu.VMEM((4, 4, XT, KB), BF),
            pltpu.VMEM((4, XT, KB), BF),
            pltpu.VMEM((NX * XT, KB), BF),
            pltpu.VMEM((2, 16, 8, 128), F32),
            pltpu.SemaphoreType.DMA((304,)),
            pltpu.SemaphoreType.DMA((304,)),
            pltpu.SemaphoreType.DMA((24,)),
        ],
        compiler_params=pltpu.CompilerParams(
            collective_id=0, has_side_effects=True, vmem_limit_bytes=60 * 2**20
        ),
        cost_estimate=pl.CostEstimate(
            flops=11_000_000_000, bytes_accessed=8_000_000, transcendentals=524288
        ),
    )(inputs, cotangent, w_up, w_down)
    mean_square = total[0, 0] / jnp.float32(2.0 * D * FF)
    scale = 1.0 / jnp.sqrt(mean_square)
    return ig, up.astype(F32) * scale, down.astype(F32) * scale, mean_square


def solution(mesh):
    placed = (P("dp", "mp"), P("dp", "mp"), P("dp", "mp"), P("mp", "dp"))
    return jax.shard_map(
        on_device,
        mesh=mesh,
        in_specs=placed,
        out_specs=(P("dp", "mp"), P("dp", "mp"), P("mp", "dp"), P()),
        check_vma=False,
    )
```

```python
import jax
import jax.numpy as jnp
from jax import lax
from jax.experimental import pallas as pl
from jax.experimental.pallas import tpu as pltpu
from jax.sharding import PartitionSpec as P

D = 4096
FF = 16384

NX, NY, NZ = 4, 4, 8
XT = 64
TZ = 2 * XT
TOK = NZ * TZ
KB = 256
UB = 128
UN = 2 * UB
ROW = NZ * KB
CUT = 768
PIECES = (0, 16, 32, 64, 96, 112, 128)

MESH = pl.DeviceIdType.MESH
BF = jnp.bfloat16
F32 = jnp.float32

root_half = 0.7071067811865476
inv_root_two_pi = 0.3989422804014327


def step(value, offset, size):
    return lax.rem(value + (offset + size), size)


def span(start, size):
    return pl.ds(pl.multiple_of(start, size), size)


def dot_nt(left, right):
    return lax.dot_general(
        left, right, (((1,), (1,)), ((), ())), preferred_element_type=F32
    )


def dot_nn(left, right):
    return lax.dot_general(
        left, right, (((1,), (0,)), ((), ())), preferred_element_type=F32
    )


def kernel(
    x_in, dy_in, wu_in, wd_in, ig_out, up_out, down_out, sq_out, scale_out,
    wu, ws, xy, ww, wt, wsib, hid, gact, act_t, pre, pre_t, pre_sib,
    part, r1r, r1l, r2r, r2l, red, land,
    py, y1r, y1l, y2r, y2l, ty, z_r, z_l, fz, ox, up_t, squares, nb,
    send, recv, local,
):
    dp, mp = lax.axis_index("dp"), lax.axis_index("mp")
    z, xh = lax.div(dp, 2), lax.rem(dp, 2)
    y, xl, c = lax.div(mp, 4), lax.rem(lax.div(mp, 2), 2), lax.rem(mp, 2)
    x = 2 * xh + xl

    def device(px, py_, pz, pc):
        return (pz * 2 + lax.div(px, 2), py_ * 4 + lax.rem(px, 2) * 2 + pc)

    def at_x(k):
        return device(step(x, k, NX), y, z, c)

    def at_y(k):
        return device(x, step(y, k, NY), z, c)

    def at_z(k):
        return device(x, y, step(z, k, NZ), c)

    sibling = device(x, y, z, 1 - c)

    started = []

    def push(src, dst, target):
        n = len(started)
        copy = pltpu.make_async_remote_copy(
            src_ref=src, dst_ref=dst, send_sem=send.at[n], recv_sem=recv.at[n],
            device_id=target, device_id_type=MESH,
        )
        copy.start()
        started.append(copy)
        return copy

    moved = []

    def move(src, dst):
        copy = pltpu.make_async_copy(src, dst, local.at[len(moved)])
        copy.start()
        moved.append(copy)
        return copy

    def land_all(copies):
        for copy in copies:
            copy.wait_recv()

    wu_own = move(wu_in, wu)
    wd_own = move(wd_in, ws.at[1])

    barrier = pltpu.get_barrier_semaphore()
    plane = [
        device(step(x, i, NX), step(y, j, NY), z, c)
        for i in range(NX) for j in range(NY) if i or j
    ]
    column = [
        device(x, y, step(z, k, NZ), pc)
        for k in range(NZ) for pc in (c, 1 - c) if k or pc is not c
    ]
    peers = (
        [at_x(k) for k in range(1, NX)]
        + [at_y(k) for k in range(1, NY)]
        + [at_z(k) for k in range(1, NZ)]
        + [sibling]
    )
    for peer in peers:
        pl.semaphore_signal(barrier, inc=1, device_id=peer, device_id_type=MESH)

    pl.semaphore_wait(barrier, len(peers))

    first, rest = pl.ds(0, CUT), pl.ds(CUT, 4 * KB - CUT)

    def rows(pz):
        return span(pz * TZ, TZ)

    def half(pz, which):
        return span(pz * TZ + which * XT, XT)

    def cols(pz):
        return span(pz * KB, KB)

    def tok_place(a):
        return xy.at[c, y, span(z * TZ + xh * XT, XT), span((xl * 2 + a) * KB, KB)]

    tok, tok_own = [], []
    for k in (1, 3, 2):
        px = step(x, k, NX)
        for a, source in ((0, x_in), (1, dy_in)):
            tok.append(push(source.at[span(px * XT, XT), :], tok_place(a), at_x(k)))
    for a, source in ((0, x_in), (1, dy_in)):
        tok_own.append(move(source.at[span(x * XT, XT), :], tok_place(a)))

    wu_own.wait()

    @pl.loop(0, NZ)
    def _(t):
        at = span(t * UB, UB)
        ws[0, at, :] = wu[:, at].T

    wd_own.wait()
    w_place = ww.at[x, :, :, cols(z)]
    wz = {}

    def w_send(k):
        wz[k] = push(ws.at[:, span(step(z, k, NZ) * UB, UB), :], w_place, at_z(k))

    w_send(1)
    w_send(7)
    w_own = move(ws.at[:, span(z * UB, UB), :], w_place)

    wx1, wx2 = {}, {}

    direct = (3, 5, 4)

    def w_hop1(k):
        if k:
            wz[k].wait_recv()
        piece = ww.at[x, :, :, cols(step(z, -k, NZ))]
        wx1[k] = [push(piece, piece, at_x(1)), push(piece, piece, at_x(-1))]
        if k in direct:
            wx2[k] = [push(piece, piece, at_x(2))]

    def w_hop2(k):
        land_all(wx1[k])
        if k in direct:
            return
        pz = cols(step(z, -k, NZ))
        right = ww.at[step(x, -1, NX), 0, :, pz]
        left = ww.at[step(x, 1, NX), 1, :, pz]
        wx2[k] = [push(right, right, at_x(1)), push(left, left, at_x(-1))]

    ya1, ya2, ca, cb, za, zb = {}, {}, {}, {}, {}, {}

    def ya_hop1(k):
        block = xy.at[c, y, rows(step(z, k, NZ)), first]
        ya1[k] = [push(block, block, at_y(1)), push(block, block, at_y(-1))]

    def ya_hop2(k):
        land_all(ya1[k])
        pz = step(z, k, NZ)
        right = xy.at[c, step(y, -1, NY), half(pz, 0), first]
        left = xy.at[c, step(y, 1, NY), half(pz, 1), first]
        ya2[k] = [push(right, right, at_y(1)), push(left, left, at_y(-1))]

    def ya_core(k):
        land_all(ya2[k])
        block = xy.at[c, :, rows(step(z, k, NZ)), first]
        ca[k] = push(block, block, sibling)

    def za_step(k):
        if k < 4:
            right = xy.at[c, y, rows(step(z, 1 - k, NZ)), first]
            left = xy.at[c, y, rows(step(z, k - 1, NZ)), first]
        else:
            right = xy.at[c, y, half(step(z, 1 - k, NZ), 0), first]
            left = xy.at[c, y, half(step(z, k - 1, NZ), 1), first]
        za[k] = [push(right, right, at_z(1)), push(left, left, at_z(-1))]

    def zb_step(k):
        if k < 4:
            right = xy.at[c, :, rows(step(z, 1 - k, NZ)), rest]
            left = xy.at[c, :, rows(step(z, k - 1, NZ)), rest]
        else:
            right = xy.at[c, :, half(step(z, 1 - k, NZ), 0), rest]
            left = xy.at[c, :, half(step(z, k - 1, NZ), 1), rest]
        zb[k] = [push(right, right, at_z(1)), push(left, left, at_z(-1))]

    def cb_core(k):
        block = xy.at[c, :, rows(step(z, k, NZ)), rest]
        cb[k] = push(block, block, sibling)

    def weight(which, pc, start):
        return ww[pl.ds(2 * pc, 2), which, :, span(start, KB)].reshape(UN, KB)

    def turn(k):
        land_all(wx2[k])
        pz = step(z, -k, NZ)

        @pl.loop(0, 2)
        def _(pc):
            for a in range(2):
                wt[a, pc, pz] = weight(a, pc, pz * KB).T

    pre_far = {}

    def land_blocks(ks):
        for k in ks:
            ca[k].wait_recv()
            cb[k].wait_recv()

    late = lax.div(step(z, 4, NZ), 2)

    def hidden_sums(ks, chunks):
        places = [rows(step(z, k, NZ)) for k in ks]
        size = TZ * len(ks)

        def operand(a, pc, py_):
            got = [
                jnp.concatenate(
                    [
                        xy[pc, py_, at, pl.ds((2 * n + a) * KB, KB)]
                        for n in range(2)
                    ],
                    axis=1,
                )
                for at in places
            ]
            return got[0] if len(got) == 1 else jnp.concatenate(got, axis=0)

        if chunks[0] == 1:
            hid[:size] = jnp.zeros((size, UN), F32)
            gact[:size] = jnp.zeros((size, UN), F32)

        @pl.loop(0, 2 * len(chunks))
        def _(p):
            pc = lax.rem(p, 2)
            py_ = lax.rem(late + chunks[0] + lax.div(p, 2), NY)
            for a, total in ((0, hid), (1, gact)):
                right = wt[a, pc, pl.ds(2 * py_, 2)].reshape(2 * KB, UN)
                total[:size] += dot_nn(operand(a, pc, py_), right)

    def hidden_ends(ks):
        places = [rows(step(z, k, NZ)) for k in ks]
        for n, (k, at) in enumerate(zip(ks, places)):
            pz = step(z, k, NZ)
            h = hid[n * TZ : (n + 1) * TZ]
            both = 0.5 * (1.0 + lax.erf(h * root_half))
            act = (h * both).astype(BF)
            slope = both + h * jnp.exp(-0.5 * h * h) * inv_root_two_pi
            grad = (gact[n * TZ : (n + 1) * TZ] * slope).astype(BF)
            pre[pz] = grad
            pre_t[:, at] = grad.T
            act_t[:, at] = act.T
            pre_far[k] = push(pre.at[pz], pre_sib.at[pz], sibling)

    for copy in tok_own:
        copy.wait()
    land_all(tok)
    block = xy.at[c, y, rows(z), rest]
    yb1 = [push(block, block, at_y(1)), push(block, block, at_y(-1))]
    za_step(1)
    ya_hop1(0)
    w_send(2)
    w_send(6)
    w_own.wait()
    w_hop1(0)
    w_hop1(1)
    w_hop1(7)

    land_all(yb1)
    right = xy.at[c, step(y, -1, NY), half(z, 0), rest]
    left = xy.at[c, step(y, 1, NY), half(z, 1), rest]
    yb2 = [push(right, right, at_y(1)), push(left, left, at_y(-1))]
    land_all(za[1])
    za_step(2)
    ya_hop1(1)
    ya_hop1(-1)
    ya_hop2(0)
    land_all(yb2)
    zb_step(1)
    cb_core(0)
    w_hop1(2)
    w_hop1(6)
    w_hop2(0)
    w_hop2(1)
    w_hop2(7)
    land_all(za[2])
    za_step(3)
    ya_hop1(2)
    ya_hop1(-2)
    w_send(3)
    w_send(5)
    ya_hop2(1)
    ya_hop2(-1)
    ya_core(0)
    land_all(zb[1])
    zb_step(2)
    cb_core(1)
    cb_core(-1)
    w_hop2(2)
    w_hop2(6)
    turn(0)
    turn(1)
    turn(7)
    land_all(za[3])
    za_step(4)
    w_send(4)
    ya_hop1(3)
    ya_hop1(-3)
    turn(2)
    turn(6)
    ya_hop2(2)
    ya_hop2(-2)
    ya_core(1)
    ya_core(-1)
    w_hop1(3)
    w_hop1(5)
    land_all(zb[2])
    zb_step(3)
    cb_core(2)
    cb_core(-2)
    land_all(za[4])
    ya_hop1(4)
    ya_hop2(3)
    ya_hop2(-3)
    ya_core(2)
    ya_core(-2)
    w_hop2(3)
    w_hop2(5)
    turn(3)
    turn(5)
    w_hop1(4)
    early = (0, 1, -1, 2, -2)
    land_all(zb[3])
    zb_step(4)
    cb_core(3)
    cb_core(-3)
    ya_hop2(4)
    ya_core(3)
    ya_core(-3)
    land_blocks(early)
    hidden_sums(early, (1, 2, 3))
    w_hop2(4)
    turn(4)
    w_far = push(ww.at[pl.ds(2 * (1 - c), 2), 0, :, :], wsib, sibling)
    ya_core(4)
    hidden_sums(early, (4,))
    hidden_ends(early)
    land_all(zb[4])
    cb_core(4)
    land_blocks((3, -3, 4))
    hidden_sums((3, -3, 4), (1, 2, 3, 4))
    hidden_ends((3, -3, 4))

    def grad_parts(pc, a):
        left = pre_t if a == 0 else act_t

        @pl.loop(0, NZ)
        def _(q):
            right = xy[
                pc, lax.div(q, 2), :, span((2 * lax.rem(q, 2) + a) * KB, KB)
            ]
            out = dot_nn(left[...], right).astype(BF)
            part[2 * pc, a, :, cols(q)] = out[:UB]
            part[2 * pc + 1, a, :, cols(q)] = out[UB:]

    far, nxt, prv = step(x, 2, NX), step(x, 1, NX), step(x, -1, NX)
    x1, x2, gz, gz_own = {}, {}, {}, {}

    def piece(q):
        return pl.ds(PIECES[q], PIECES[q + 1] - PIECES[q])

    def x_step1(q, a):
        src = part.at[far, a, piece(q), :]
        if a == 0:
            x1[q] = [push(src, r1r.at[piece(q), :], at_x(1))]
        else:
            x1[q].append(push(src, r1l.at[piece(q), :], at_x(-1)))

    def x_step2(q):
        land_all(x1[q])
        at = piece(q)
        for px, a, got in ((nxt, 0, r1r), (prv, 1, r1l)):
            total = part[px, a, at, :].astype(F32) + got[at, :].astype(F32)
            part[px, a, at, :] = total.astype(BF)
        x2[q] = [
            push(part.at[nxt, :, at, :], r2r.at[:, at, :], at_x(1)),
            push(part.at[prv, :, at, :], r2l.at[:, at, :], at_x(-1)),
        ]

    def x_sum(q):
        land_all(x2[q])
        at = piece(q)
        for a in range(2):
            total = (
                part[x, a, at, :].astype(F32)
                + r2r[a, at, :].astype(F32)
                + r2l[a, at, :].astype(F32)
            ).astype(BF)
            red[a, at, :] = total
            v = total.astype(F32)
            squares[...] += jnp.sum(v * v, axis=0, keepdims=True)

    def x_spread(q):
        at = piece(q)
        place = land.at[:, pl.ds(pl.multiple_of(z * UB + PIECES[q], 16), at.size), :]
        gz[q] = [
            push(red.at[:, at, cols(step(z, k, NZ))], place, at_z(k))
            for k in (1, 7, 2, 6, 3, 5, 4)
        ]
        gz_own[q] = move(red.at[:, at, cols(z)], place)

    def x_step3(q):
        x_sum(q)
        x_spread(q)

    pieces = (2, 1, 3, 0)
    size = NZ * XT

    def ig_own(py_, j):
        px = step(x, pieces[j], NX)
        tokens = span(lax.div(px, 2) * XT, XT)
        start = (2 * py_ + lax.rem(px, 2)) * KB
        near = weight(0, c, start)
        other = wsib[:, :, span(start, KB)].reshape(UN, KB)
        return dot_nn(pre[:, tokens, :].reshape(size, UN), near) + dot_nn(
            pre_sib[:, tokens, :].reshape(size, UN), other
        )

    y1, y2 = {}, {}
    low, high = pl.ds(0, size // 2), pl.ds(size // 2, size // 2)

    def y_step1(j):
        py[0, j] = ig_own(step(y, 2, NY), j).astype(BF)
        y1[j] = [
            push(py.at[0, j, low, :], y1r.at[j], at_y(1)),
            push(py.at[0, j, high, :], y1l.at[j], at_y(-1)),
        ]

    def y_step2(j):
        total = ig_own(step(y, 1, NY), j)
        y1[j][0].wait_recv()
        py[1, j, low, :] = (total[: size // 2] + y1r[j].astype(F32)).astype(BF)
        py[1, j, high, :] = total[size // 2 :].astype(BF)
        right = push(py.at[1, j], y2r.at[j], at_y(1))
        total = ig_own(step(y, -1, NY), j)
        y1[j][1].wait_recv()
        py[2, j, low, :] = total[: size // 2].astype(BF)
        py[2, j, high, :] = (total[size // 2 :] + y1l[j].astype(F32)).astype(BF)
        y2[j] = [right, push(py.at[2, j], y2l.at[j], at_y(-1))]

    def y_step3(j):
        total = ig_own(y, j)
        land_all(y2[j])
        ty[j] = (total + y2r[j].astype(F32) + y2l[j].astype(F32)).astype(BF)

    iz = {}
    XH = XT // 2

    def band(pz):
        return span(pz * XT, XT)

    def part_band(pz, which):
        return span(pz * XT + which * XH, XH)

    def z_step(j, k):
        right, left = step(z, 5 - k, NZ), step(z, k - 5, NZ)
        if k == 1:
            iz[j, 1] = [
                push(ty.at[j, part_band(right, 0), :], z_r.at[j, 0, pl.ds(0, XH), :], at_z(1)),
                push(ty.at[j, part_band(left, 1), :], z_l.at[j, 0, pl.ds(XH, XH), :], at_z(-1)),
            ]
            return
        land_all(iz[j, k - 1])
        if k == 2:
            add_r, add_l = part_band(right, 0), part_band(left, 1)
            got_r, got_l = z_r[j, 0, :XH], z_l[j, 0, XH:]
        else:
            add_r, add_l = band(right), band(left)
            got_r, got_l = z_r[j, k - 2], z_l[j, k - 2]
        for at, got in ((add_r, got_r), (add_l, got_l)):
            ty[j, at, :] = (ty[j, at, :].astype(F32) + got.astype(F32)).astype(BF)
        iz[j, k] = [
            push(ty.at[j, band(right), :], z_r.at[j, k - 1], at_z(1)),
            push(ty.at[j, band(left), :], z_l.at[j, k - 1], at_z(-1)),
        ]

    far_out = []

    def z_last(j):
        land_all(iz[j, 4])
        total = (
            ty[j, band(z), :].astype(F32)
            + z_r[j, 3].astype(F32)
            + z_l[j, 3].astype(F32)
        ).astype(BF)
        if pieces[j]:
            fz[j] = total
            far_out.append(
                push(fz.at[j], ox.at[span(x * XT, XT), :], at_x(pieces[j]))
            )
        else:
            ox[span(x * XT, XT), :] = total

    squares[...] = jnp.zeros_like(squares)
    grad_parts(1 - xh, 0)
    for q in range(4):
        x_step1(q, 0)
    for k in pre_far:
        pre_far[k].wait_recv()
    w_far.wait_recv()
    y_step1(0)
    y_step1(1)
    grad_parts(1 - xh, 1)
    for q in range(4):
        x_step1(q, 1)
    y_step1(2)
    grad_parts(xh, 0)
    grad_parts(xh, 1)
    x_step2(0)
    x_step2(1)
    y_step2(0)
    x_step2(2)
    y_step1(3)
    y_step2(1)
    for q in (4, 5):
        x_step1(q, 0)
        x_step1(q, 1)
    x_step3(0)
    y_step2(2)
    x_step3(1)
    y_step3(0)
    z_step(0, 1)
    x_step2(3)
    y_step2(3)
    x_step3(2)
    y_step3(1)
    z_step(1, 1)
    z_step(0, 2)
    x_step2(4)
    x_step2(5)
    y_step3(2)
    z_step(2, 1)
    z_step(1, 2)
    z_step(0, 3)
    x_step3(3)
    z_step(2, 2)
    y_step3(3)
    z_step(3, 1)
    x_sum(4)
    x_sum(5)

    value = jnp.sum(squares[...], axis=1, keepdims=True)

    def exchange(stage, me, targets, value):
        nb[stage, me] = jnp.broadcast_to(value, (8, 128))
        return [push(nb.at[stage, me], nb.at[stage, me], t) for t in targets]

    def collect(stage, copies):
        land_all(copies)
        total = nb[stage, 0]
        for n in range(1, 16):
            total = total + nb[stage, n]
        return total[:1, :1]

    norm = exchange(0, 2 * z + c, column, value)
    z_step(1, 3)
    z_step(2, 3)
    x_spread(4)
    x_spread(5)
    z_step(3, 2)
    z_step(0, 4)
    z_step(1, 4)
    z_step(2, 4)
    value = collect(0, norm)
    norm = exchange(1, 4 * x + y, plane, value)
    z_step(3, 3)
    z_last(0)
    z_last(1)
    z_last(2)
    z_step(3, 4)
    for q in gz:
        gz_own[q].wait()
        land_all(gz[q])
    down_copy = move(land.at[1], down_out)

    @pl.loop(0, NZ)
    def _(t):
        at = span(t * UB, UB)
        up_t[:, at] = land[0, at, :].T

    up_copy = move(up_t, up_out)
    value = collect(1, norm)
    sq_out[0, 0] = jnp.max(value)
    scale_out[0, 0] = jnp.max(1.0 / jnp.sqrt(value / (2.0 * D * FF)))
    z_last(3)
    land_all(far_out)
    ig_out[...] = ox[...]
    down_copy.wait()
    up_copy.wait()

    for copy in started:
        copy.wait_send()


def on_device(inputs, cotangent, w_up, w_down):
    vmem = pl.BlockSpec(memory_space=pltpu.VMEM)
    hbm = pl.BlockSpec(memory_space=pl.ANY)
    smem = pl.BlockSpec(memory_space=pltpu.SMEM)
    ig, up, down, total, scale = pl.pallas_call(
        kernel,
        out_shape=(
            jax.ShapeDtypeStruct((NX * XT, KB), BF),
            jax.ShapeDtypeStruct((KB, NZ * UB), BF),
            jax.ShapeDtypeStruct((NZ * UB, KB), BF),
            jax.ShapeDtypeStruct((1, 1), F32),
            jax.ShapeDtypeStruct((1, 1), F32),
        ),
        in_specs=[hbm] * 4,
        out_specs=(vmem, hbm, hbm, smem, smem),
        scratch_shapes=[
            pltpu.VMEM((KB, NZ * UB), BF),
            pltpu.VMEM((2, NZ * UB, KB), BF),
            pltpu.VMEM((2, NY, TOK, 4 * KB), BF),
            pltpu.VMEM((NX, 2, UB, ROW), BF),
            pltpu.VMEM((2, 2, NZ, KB, UN), BF),
            pltpu.VMEM((2, UB, ROW), BF),
            pltpu.VMEM((5 * TZ, UN), F32),
            pltpu.VMEM((5 * TZ, UN), F32),
            pltpu.VMEM((UN, TOK), BF),
            pltpu.VMEM((NZ, TZ, UN), BF),
            pltpu.VMEM((UN, TOK), BF),
            pltpu.VMEM((NZ, TZ, UN), BF),
            pltpu.VMEM((NX, 2, UB, ROW), BF),
            pltpu.VMEM((UB, ROW), BF),
            pltpu.VMEM((UB, ROW), BF),
            pltpu.VMEM((2, UB, ROW), BF),
            pltpu.VMEM((2, UB, ROW), BF),
            pltpu.VMEM((2, UB, ROW), BF),
            pltpu.VMEM((2, NZ * UB, KB), BF),
            pltpu.VMEM((3, 4, NZ * XT, KB), BF),
            pltpu.VMEM((4, NZ * XT // 2, KB), BF),
            pltpu.VMEM((4, NZ * XT // 2, KB), BF),
            pltpu.VMEM((4, NZ * XT, KB), BF),
            pltpu.VMEM((4, NZ * XT, KB), BF),
            pltpu.VMEM((4, NZ * XT, KB), BF),
            pltpu.VMEM((4, 4, XT, KB), BF),
            pltpu.VMEM((4, 4, XT, KB), BF),
            pltpu.VMEM((4, XT, KB), BF),
            pltpu.VMEM((NX * XT, KB), BF),
            pltpu.VMEM((KB, NZ * UB), BF),
            pltpu.VMEM((1, ROW), F32),
            pltpu.VMEM((2, 16, 8, 128), F32),
            pltpu.SemaphoreType.DMA((304,)),
            pltpu.SemaphoreType.DMA((304,)),
            pltpu.SemaphoreType.DMA((24,)),
        ],
        compiler_params=pltpu.CompilerParams(
            collective_id=0, has_side_effects=True, vmem_limit_bytes=60 * 2**20
        ),
        cost_estimate=pl.CostEstimate(
            flops=11_000_000_000, bytes_accessed=8_000_000, transcendentals=524288
        ),
    )(inputs, cotangent, w_up, w_down)
    mean_square = total[0, 0] / jnp.float32(2.0 * D * FF)
    scale = scale[0, 0]
    return ig, up.astype(F32) * scale, down.astype(F32) * scale, mean_square


def solution(mesh):
    placed = (P("dp", "mp"), P("dp", "mp"), P("dp", "mp"), P("mp", "dp"))
    return jax.shard_map(
        on_device,
        mesh=mesh,
        in_specs=placed,
        out_specs=(P("dp", "mp"), P("dp", "mp"), P("mp", "dp"), P()),
        check_vma=False,
    )
```

```python
import jax
import jax.numpy as jnp
from jax import lax
from jax.experimental import pallas as pl
from jax.experimental.pallas import tpu as pltpu
from jax.sharding import PartitionSpec as P

D = 4096
FF = 16384

NX, NY, NZ = 4, 4, 8
XT = 64
TZ = 2 * XT
TOK = NZ * TZ
KB = 256
UB = 128
UN = 2 * UB
ROW = NZ * KB
CUT = 768
PIECES = (0, 16, 32, 64, 96, 112, 128)

MESH = pl.DeviceIdType.MESH
BF = jnp.bfloat16
F32 = jnp.float32

root_half = 0.7071067811865476
inv_root_two_pi = 0.3989422804014327


def step(value, offset, size):
    return lax.rem(value + (offset + size), size)


def span(start, size):
    return pl.ds(pl.multiple_of(start, size), size)


def dot_nt(left, right):
    return lax.dot_general(
        left, right, (((1,), (1,)), ((), ())), preferred_element_type=F32
    )


def dot_nn(left, right):
    return lax.dot_general(
        left, right, (((1,), (0,)), ((), ())), preferred_element_type=F32
    )


def kernel(
    x_in, dy_in, wu_in, wd_in, ig_out, up_out, down_out, sq_out,
    wu, ws, xy, ww, wt, wsib, hid, gact, act_t, pre, pre_t, pre_sib,
    part, r1r, r1l, r2r, r2l, red, land,
    py, y1r, y1l, y2r, y2l, ty, z_r, z_l, fz, ox, up_t, squares, nb,
    send, recv, local,
):
    dp, mp = lax.axis_index("dp"), lax.axis_index("mp")
    z, xh = lax.div(dp, 2), lax.rem(dp, 2)
    y, xl, c = lax.div(mp, 4), lax.rem(lax.div(mp, 2), 2), lax.rem(mp, 2)
    x = 2 * xh + xl

    def device(px, py_, pz, pc):
        return (pz * 2 + lax.div(px, 2), py_ * 4 + lax.rem(px, 2) * 2 + pc)

    def at_x(k):
        return device(step(x, k, NX), y, z, c)

    def at_y(k):
        return device(x, step(y, k, NY), z, c)

    def at_z(k):
        return device(x, y, step(z, k, NZ), c)

    sibling = device(x, y, z, 1 - c)

    started = []

    def push(src, dst, target):
        n = len(started)
        copy = pltpu.make_async_remote_copy(
            src_ref=src, dst_ref=dst, send_sem=send.at[n], recv_sem=recv.at[n],
            device_id=target, device_id_type=MESH,
        )
        copy.start()
        started.append(copy)
        return copy

    moved = []

    def move(src, dst):
        copy = pltpu.make_async_copy(src, dst, local.at[len(moved)])
        copy.start()
        moved.append(copy)
        return copy

    def land_all(copies):
        for copy in copies:
            copy.wait_recv()

    wu_own = move(wu_in, wu)
    wd_own = move(wd_in, ws.at[1])

    barrier = pltpu.get_barrier_semaphore()
    plane = [
        device(step(x, i, NX), step(y, j, NY), z, c)
        for i in range(NX) for j in range(NY) if i or j
    ]
    column = [
        device(x, y, step(z, k, NZ), pc)
        for k in range(NZ) for pc in (c, 1 - c) if k or pc is not c
    ]
    peers = (
        [at_x(k) for k in range(1, NX)]
        + [at_y(k) for k in range(1, NY)]
        + [at_z(k) for k in range(1, NZ)]
        + [sibling]
    )
    for peer in peers:
        pl.semaphore_signal(barrier, inc=1, device_id=peer, device_id_type=MESH)

    pl.semaphore_wait(barrier, len(peers))

    first, rest = pl.ds(0, CUT), pl.ds(CUT, 4 * KB - CUT)

    def rows(pz):
        return span(pz * TZ, TZ)

    def half(pz, which):
        return span(pz * TZ + which * XT, XT)

    def cols(pz):
        return span(pz * KB, KB)

    def tok_place(a):
        return xy.at[c, y, span(z * TZ + xh * XT, XT), span((xl * 2 + a) * KB, KB)]

    tok, tok_own = [], []
    for k in (1, 3, 2):
        px = step(x, k, NX)
        for a, source in ((0, x_in), (1, dy_in)):
            tok.append(push(source.at[span(px * XT, XT), :], tok_place(a), at_x(k)))
    for a, source in ((0, x_in), (1, dy_in)):
        tok_own.append(move(source.at[span(x * XT, XT), :], tok_place(a)))

    wu_own.wait()

    @pl.loop(0, NZ)
    def _(t):
        at = span(t * UB, UB)
        ws[0, at, :] = wu[:, at].T

    wd_own.wait()
    w_place = ww.at[x, :, :, cols(z)]
    wz = {}

    def w_send(k):
        wz[k] = push(ws.at[:, span(step(z, k, NZ) * UB, UB), :], w_place, at_z(k))

    w_send(1)
    w_send(7)
    w_own = move(ws.at[:, span(z * UB, UB), :], w_place)

    wx1, wx2 = {}, {}

    direct = (3, 5, 4)

    def w_hop1(k):
        if k:
            wz[k].wait_recv()
        piece = ww.at[x, :, :, cols(step(z, -k, NZ))]
        wx1[k] = [push(piece, piece, at_x(1)), push(piece, piece, at_x(-1))]
        if k in direct:
            wx2[k] = [push(piece, piece, at_x(2))]

    def w_hop2(k):
        land_all(wx1[k])
        if k in direct:
            return
        pz = cols(step(z, -k, NZ))
        right = ww.at[step(x, -1, NX), 0, :, pz]
        left = ww.at[step(x, 1, NX), 1, :, pz]
        wx2[k] = [push(right, right, at_x(1)), push(left, left, at_x(-1))]

    ya1, ya2, ca, cb, za, zb = {}, {}, {}, {}, {}, {}

    def ya_hop1(k):
        block = xy.at[c, y, rows(step(z, k, NZ)), first]
        ya1[k] = [push(block, block, at_y(1)), push(block, block, at_y(-1))]

    def ya_hop2(k):
        land_all(ya1[k])
        pz = step(z, k, NZ)
        right = xy.at[c, step(y, -1, NY), half(pz, 0), first]
        left = xy.at[c, step(y, 1, NY), half(pz, 1), first]
        ya2[k] = [push(right, right, at_y(1)), push(left, left, at_y(-1))]

    def ya_core(k):
        land_all(ya2[k])
        block = xy.at[c, :, rows(step(z, k, NZ)), first]
        ca[k] = push(block, block, sibling)

    def za_step(k):
        if k < 4:
            right = xy.at[c, y, rows(step(z, 1 - k, NZ)), first]
            left = xy.at[c, y, rows(step(z, k - 1, NZ)), first]
        else:
            right = xy.at[c, y, half(step(z, 1 - k, NZ), 0), first]
            left = xy.at[c, y, half(step(z, k - 1, NZ), 1), first]
        za[k] = [push(right, right, at_z(1)), push(left, left, at_z(-1))]

    def zb_step(k):
        if k < 4:
            right = xy.at[c, :, rows(step(z, 1 - k, NZ)), rest]
            left = xy.at[c, :, rows(step(z, k - 1, NZ)), rest]
        else:
            right = xy.at[c, :, half(step(z, 1 - k, NZ), 0), rest]
            left = xy.at[c, :, half(step(z, k - 1, NZ), 1), rest]
        zb[k] = [push(right, right, at_z(1)), push(left, left, at_z(-1))]

    def cb_core(k):
        block = xy.at[c, :, rows(step(z, k, NZ)), rest]
        cb[k] = push(block, block, sibling)

    def weight(which, pc, start):
        return ww[pl.ds(2 * pc, 2), which, :, span(start, KB)].reshape(UN, KB)

    def turn(k):
        land_all(wx2[k])
        pz = step(z, -k, NZ)

        @pl.loop(0, 2)
        def _(pc):
            for a in range(2):
                wt[a, pc, pz] = weight(a, pc, pz * KB).T

    pre_far = {}

    def land_blocks(ks):
        for k in ks:
            ca[k].wait_recv()
            cb[k].wait_recv()

    late = lax.div(step(z, 4, NZ), 2)

    def hidden_sums(ks, chunks):
        places = [rows(step(z, k, NZ)) for k in ks]
        size = TZ * len(ks)

        def operand(a, pc, py_):
            got = [
                jnp.concatenate(
                    [
                        xy[pc, py_, at, pl.ds((2 * n + a) * KB, KB)]
                        for n in range(2)
                    ],
                    axis=1,
                )
                for at in places
            ]
            return got[0] if len(got) == 1 else jnp.concatenate(got, axis=0)

        if chunks[0] == 1:
            hid[:size] = jnp.zeros((size, UN), F32)
            gact[:size] = jnp.zeros((size, UN), F32)

        @pl.loop(0, 2 * len(chunks), unroll=2)
        def _(p):
            pc = lax.rem(p, 2)
            py_ = lax.rem(late + chunks[0] + lax.div(p, 2), NY)
            for a, total in ((0, hid), (1, gact)):
                right = wt[a, pc, pl.ds(2 * py_, 2)].reshape(2 * KB, UN)
                total[:size] += dot_nn(operand(a, pc, py_), right)

    def hidden_ends(ks):
        places = [rows(step(z, k, NZ)) for k in ks]
        for n, (k, at) in enumerate(zip(ks, places)):
            pz = step(z, k, NZ)
            h = hid[n * TZ : (n + 1) * TZ]
            both = 0.5 * (1.0 + lax.erf(h * root_half))
            act = (h * both).astype(BF)
            slope = both + h * jnp.exp(-0.5 * h * h) * inv_root_two_pi
            grad = (gact[n * TZ : (n + 1) * TZ] * slope).astype(BF)
            pre[pz] = grad
            pre_t[:, at] = grad.T
            act_t[:, at] = act.T
            pre_far[k] = push(pre.at[pz], pre_sib.at[pz], sibling)

    for copy in tok_own:
        copy.wait()
    land_all(tok)
    block = xy.at[c, y, rows(z), rest]
    yb1 = [push(block, block, at_y(1)), push(block, block, at_y(-1))]
    za_step(1)
    ya_hop1(0)
    w_send(2)
    w_send(6)
    w_own.wait()
    w_hop1(0)
    w_hop1(1)
    w_hop1(7)

    land_all(yb1)
    right = xy.at[c, step(y, -1, NY), half(z, 0), rest]
    left = xy.at[c, step(y, 1, NY), half(z, 1), rest]
    yb2 = [push(right, right, at_y(1)), push(left, left, at_y(-1))]
    land_all(za[1])
    za_step(2)
    ya_hop1(1)
    ya_hop1(-1)
    ya_hop2(0)
    land_all(yb2)
    zb_step(1)
    cb_core(0)
    w_hop1(2)
    w_hop1(6)
    w_hop2(0)
    w_hop2(1)
    w_hop2(7)
    land_all(za[2])
    za_step(3)
    ya_hop1(2)
    ya_hop1(-2)
    w_send(3)
    w_send(5)
    ya_hop2(1)
    ya_hop2(-1)
    ya_core(0)
    land_all(zb[1])
    zb_step(2)
    cb_core(1)
    cb_core(-1)
    w_hop2(2)
    w_hop2(6)
    turn(0)
    turn(1)
    turn(7)
    land_all(za[3])
    za_step(4)
    w_send(4)
    ya_hop1(3)
    ya_hop1(-3)
    turn(2)
    turn(6)
    ya_hop2(2)
    ya_hop2(-2)
    ya_core(1)
    ya_core(-1)
    w_hop1(3)
    w_hop1(5)
    land_all(zb[2])
    zb_step(3)
    cb_core(2)
    cb_core(-2)
    land_all(za[4])
    ya_hop1(4)
    ya_hop2(3)
    ya_hop2(-3)
    ya_core(2)
    ya_core(-2)
    w_hop2(3)
    w_hop2(5)
    turn(3)
    turn(5)
    w_hop1(4)
    early = (0, 1, -1, 2, -2)
    land_all(zb[3])
    zb_step(4)
    cb_core(3)
    cb_core(-3)
    ya_hop2(4)
    ya_core(3)
    ya_core(-3)
    land_blocks(early)
    hidden_sums(early, (1, 2, 3))
    w_hop2(4)
    turn(4)
    w_far = push(ww.at[pl.ds(2 * (1 - c), 2), 0, :, :], wsib, sibling)
    ya_core(4)
    hidden_sums(early, (4,))
    hidden_ends(early)
    land_all(zb[4])
    cb_core(4)
    land_blocks((3, -3, 4))
    hidden_sums((3, -3, 4), (1, 2, 3, 4))
    hidden_ends((3, -3, 4))

    def grad_parts(pc, a):
        left = pre_t if a == 0 else act_t

        @pl.loop(0, NZ, unroll=4)
        def _(q):
            right = xy[
                pc, lax.div(q, 2), :, span((2 * lax.rem(q, 2) + a) * KB, KB)
            ]
            out = dot_nn(left[...], right).astype(BF)
            part[2 * pc, a, :, cols(q)] = out[:UB]
            part[2 * pc + 1, a, :, cols(q)] = out[UB:]

    far, nxt, prv = step(x, 2, NX), step(x, 1, NX), step(x, -1, NX)
    x1, x2, gz, gz_own = {}, {}, {}, {}

    def piece(q):
        return pl.ds(PIECES[q], PIECES[q + 1] - PIECES[q])

    def x_step1(q, a):
        src = part.at[far, a, piece(q), :]
        if a == 0:
            x1[q] = [push(src, r1r.at[piece(q), :], at_x(1))]
        else:
            x1[q].append(push(src, r1l.at[piece(q), :], at_x(-1)))

    def x_step2(q):
        land_all(x1[q])
        at = piece(q)
        for px, a, got in ((nxt, 0, r1r), (prv, 1, r1l)):
            total = part[px, a, at, :].astype(F32) + got[at, :].astype(F32)
            part[px, a, at, :] = total.astype(BF)
        x2[q] = [
            push(part.at[nxt, :, at, :], r2r.at[:, at, :], at_x(1)),
            push(part.at[prv, :, at, :], r2l.at[:, at, :], at_x(-1)),
        ]

    def x_sum(q):
        land_all(x2[q])
        at = piece(q)
        for a in range(2):
            total = (
                part[x, a, at, :].astype(F32)
                + r2r[a, at, :].astype(F32)
                + r2l[a, at, :].astype(F32)
            ).astype(BF)
            red[a, at, :] = total
            v = total.astype(F32)
            squares[...] += jnp.sum(v * v, axis=0, keepdims=True)

    def x_spread(q):
        at = piece(q)
        place = land.at[:, pl.ds(pl.multiple_of(z * UB + PIECES[q], 16), at.size), :]
        gz[q] = [
            push(red.at[:, at, cols(step(z, k, NZ))], place, at_z(k))
            for k in (1, 7, 2, 6, 3, 5, 4)
        ]
        gz_own[q] = move(red.at[:, at, cols(z)], place)

    def x_step3(q):
        x_sum(q)
        x_spread(q)

    pieces = (2, 1, 3, 0)
    size = NZ * XT

    def ig_own(py_, j):
        px = step(x, pieces[j], NX)
        tokens = span(lax.div(px, 2) * XT, XT)
        start = (2 * py_ + lax.rem(px, 2)) * KB
        near = weight(0, c, start)
        other = wsib[:, :, span(start, KB)].reshape(UN, KB)
        return dot_nn(pre[:, tokens, :].reshape(size, UN), near) + dot_nn(
            pre_sib[:, tokens, :].reshape(size, UN), other
        )

    y1, y2 = {}, {}
    low, high = pl.ds(0, size // 2), pl.ds(size // 2, size // 2)

    def y_step1(j):
        py[0, j] = ig_own(step(y, 2, NY), j).astype(BF)
        y1[j] = [
            push(py.at[0, j, low, :], y1r.at[j], at_y(1)),
            push(py.at[0, j, high, :], y1l.at[j], at_y(-1)),
        ]

    def y_step2(j):
        total = ig_own(step(y, 1, NY), j)
        y1[j][0].wait_recv()
        py[1, j, low, :] = (total[: size // 2] + y1r[j].astype(F32)).astype(BF)
        py[1, j, high, :] = total[size // 2 :].astype(BF)
        right = push(py.at[1, j], y2r.at[j], at_y(1))
        total = ig_own(step(y, -1, NY), j)
        y1[j][1].wait_recv()
        py[2, j, low, :] = total[: size // 2].astype(BF)
        py[2, j, high, :] = (total[size // 2 :] + y1l[j].astype(F32)).astype(BF)
        y2[j] = [right, push(py.at[2, j], y2l.at[j], at_y(-1))]

    def y_step3(j):
        total = ig_own(y, j)
        land_all(y2[j])
        ty[j] = (total + y2r[j].astype(F32) + y2l[j].astype(F32)).astype(BF)

    iz = {}
    XH = XT // 2

    def band(pz):
        return span(pz * XT, XT)

    def part_band(pz, which):
        return span(pz * XT + which * XH, XH)

    def z_step(j, k):
        right, left = step(z, 5 - k, NZ), step(z, k - 5, NZ)
        if k == 1:
            iz[j, 1] = [
                push(ty.at[j, part_band(right, 0), :], z_r.at[j, 0, pl.ds(0, XH), :], at_z(1)),
                push(ty.at[j, part_band(left, 1), :], z_l.at[j, 0, pl.ds(XH, XH), :], at_z(-1)),
            ]
            return
        land_all(iz[j, k - 1])
        if k == 2:
            add_r, add_l = part_band(right, 0), part_band(left, 1)
            got_r, got_l = z_r[j, 0, :XH], z_l[j, 0, XH:]
        else:
            add_r, add_l = band(right), band(left)
            got_r, got_l = z_r[j, k - 2], z_l[j, k - 2]
        for at, got in ((add_r, got_r), (add_l, got_l)):
            ty[j, at, :] = (ty[j, at, :].astype(F32) + got.astype(F32)).astype(BF)
        iz[j, k] = [
            push(ty.at[j, band(right), :], z_r.at[j, k - 1], at_z(1)),
            push(ty.at[j, band(left), :], z_l.at[j, k - 1], at_z(-1)),
        ]

    far_out = []

    def z_last(j):
        land_all(iz[j, 4])
        total = (
            ty[j, band(z), :].astype(F32)
            + z_r[j, 3].astype(F32)
            + z_l[j, 3].astype(F32)
        ).astype(BF)
        if pieces[j]:
            fz[j] = total
            far_out.append(
                push(fz.at[j], ox.at[span(x * XT, XT), :], at_x(pieces[j]))
            )
        else:
            ox[span(x * XT, XT), :] = total

    squares[...] = jnp.zeros_like(squares)
    grad_parts(1 - xh, 0)
    for q in range(4):
        x_step1(q, 0)
    for k in pre_far:
        pre_far[k].wait_recv()
    w_far.wait_recv()
    y_step1(0)
    y_step1(1)
    grad_parts(1 - xh, 1)
    for q in range(4):
        x_step1(q, 1)
    y_step1(2)
    grad_parts(xh, 0)
    grad_parts(xh, 1)
    x_step2(0)
    x_step2(1)
    y_step2(0)
    x_step2(2)
    y_step1(3)
    y_step2(1)
    for q in (4, 5):
        x_step1(q, 0)
        x_step1(q, 1)
    x_step3(0)
    y_step2(2)
    x_step3(1)
    y_step3(0)
    z_step(0, 1)
    x_step2(3)
    y_step2(3)
    x_step3(2)
    y_step3(1)
    z_step(1, 1)
    z_step(0, 2)
    x_step2(4)
    x_step2(5)
    y_step3(2)
    z_step(2, 1)
    z_step(1, 2)
    z_step(0, 3)
    x_step3(3)
    z_step(2, 2)
    y_step3(3)
    z_step(3, 1)
    x_sum(4)
    x_sum(5)

    value = jnp.sum(squares[...], axis=1, keepdims=True)

    def exchange(stage, me, targets, value):
        nb[stage, me] = jnp.broadcast_to(value, (8, 128))
        return [push(nb.at[stage, me], nb.at[stage, me], t) for t in targets]

    def collect(stage, copies):
        land_all(copies)
        total = nb[stage, 0]
        for n in range(1, 16):
            total = total + nb[stage, n]
        return total[:1, :1]

    norm = exchange(0, 2 * z + c, column, value)
    z_step(1, 3)
    z_step(2, 3)
    x_spread(4)
    x_spread(5)
    z_step(3, 2)
    z_step(0, 4)
    z_step(1, 4)
    z_step(2, 4)
    value = collect(0, norm)
    norm = exchange(1, 4 * x + y, plane, value)
    z_step(3, 3)
    z_last(0)
    z_last(1)
    z_last(2)
    z_step(3, 4)
    for q in gz:
        gz_own[q].wait()
        land_all(gz[q])
    down_copy = move(land.at[1], down_out)

    @pl.loop(0, NZ)
    def _(t):
        at = span(t * UB, UB)
        up_t[:, at] = land[0, at, :].T

    up_copy = move(up_t, up_out)
    value = collect(1, norm)
    sq_out[0, 0] = jnp.max(value)
    z_last(3)
    land_all(far_out)
    ig_out[...] = ox[...]
    down_copy.wait()
    up_copy.wait()

    for copy in started:
        copy.wait_send()


def on_device(inputs, cotangent, w_up, w_down):
    vmem = pl.BlockSpec(memory_space=pltpu.VMEM)
    hbm = pl.BlockSpec(memory_space=pl.ANY)
    smem = pl.BlockSpec(memory_space=pltpu.SMEM)
    ig, up, down, total = pl.pallas_call(
        kernel,
        out_shape=(
            jax.ShapeDtypeStruct((NX * XT, KB), BF),
            jax.ShapeDtypeStruct((KB, NZ * UB), BF),
            jax.ShapeDtypeStruct((NZ * UB, KB), BF),
            jax.ShapeDtypeStruct((1, 1), F32),
        ),
        in_specs=[hbm] * 4,
        out_specs=(vmem, hbm, hbm, smem),
        scratch_shapes=[
            pltpu.VMEM((KB, NZ * UB), BF),
            pltpu.VMEM((2, NZ * UB, KB), BF),
            pltpu.VMEM((2, NY, TOK, 4 * KB), BF),
            pltpu.VMEM((NX, 2, UB, ROW), BF),
            pltpu.VMEM((2, 2, NZ, KB, UN), BF),
            pltpu.VMEM((2, UB, ROW), BF),
            pltpu.VMEM((5 * TZ, UN), F32),
            pltpu.VMEM((5 * TZ, UN), F32),
            pltpu.VMEM((UN, TOK), BF),
            pltpu.VMEM((NZ, TZ, UN), BF),
            pltpu.VMEM((UN, TOK), BF),
            pltpu.VMEM((NZ, TZ, UN), BF),
            pltpu.VMEM((NX, 2, UB, ROW), BF),
            pltpu.VMEM((UB, ROW), BF),
            pltpu.VMEM((UB, ROW), BF),
            pltpu.VMEM((2, UB, ROW), BF),
            pltpu.VMEM((2, UB, ROW), BF),
            pltpu.VMEM((2, UB, ROW), BF),
            pltpu.VMEM((2, NZ * UB, KB), BF),
            pltpu.VMEM((3, 4, NZ * XT, KB), BF),
            pltpu.VMEM((4, NZ * XT // 2, KB), BF),
            pltpu.VMEM((4, NZ * XT // 2, KB), BF),
            pltpu.VMEM((4, NZ * XT, KB), BF),
            pltpu.VMEM((4, NZ * XT, KB), BF),
            pltpu.VMEM((4, NZ * XT, KB), BF),
            pltpu.VMEM((4, 4, XT, KB), BF),
            pltpu.VMEM((4, 4, XT, KB), BF),
            pltpu.VMEM((4, XT, KB), BF),
            pltpu.VMEM((NX * XT, KB), BF),
            pltpu.VMEM((KB, NZ * UB), BF),
            pltpu.VMEM((1, ROW), F32),
            pltpu.VMEM((2, 16, 8, 128), F32),
            pltpu.SemaphoreType.DMA((304,)),
            pltpu.SemaphoreType.DMA((304,)),
            pltpu.SemaphoreType.DMA((24,)),
        ],
        compiler_params=pltpu.CompilerParams(
            collective_id=0, has_side_effects=True, vmem_limit_bytes=60 * 2**20
        ),
        cost_estimate=pl.CostEstimate(
            flops=11_000_000_000, bytes_accessed=8_000_000, transcendentals=524288
        ),
    )(inputs, cotangent, w_up, w_down)
    mean_square = total[0, 0] / jnp.float32(2.0 * D * FF)
    scale = 1.0 / jnp.sqrt(mean_square)
    return ig, up.astype(F32) * scale, down.astype(F32) * scale, mean_square


def solution(mesh):
    placed = (P("dp", "mp"), P("dp", "mp"), P("dp", "mp"), P("mp", "dp"))
    return jax.shard_map(
        on_device,
        mesh=mesh,
        in_specs=placed,
        out_specs=(P("dp", "mp"), P("dp", "mp"), P("mp", "dp"), P()),
        check_vma=False,
    )
```

```python
import jax
import jax.numpy as jnp
from jax import lax
from jax.experimental import pallas as pl
from jax.experimental.pallas import tpu as pltpu
from jax.sharding import PartitionSpec as P

D = 4096
FF = 16384

NX, NY, NZ = 4, 4, 8
XT = 64
TZ = 2 * XT
TOK = NZ * TZ
KB = 256
UB = 128
UN = 2 * UB
ROW = NZ * KB
CUT = 768
PIECES = (0, 16, 32, 64, 96, 112, 128)

MESH = pl.DeviceIdType.MESH
BF = jnp.bfloat16
F32 = jnp.float32

root_half = 0.7071067811865476
inv_root_two_pi = 0.3989422804014327


def step(value, offset, size):
    return lax.rem(value + (offset + size), size)


def span(start, size):
    return pl.ds(pl.multiple_of(start, size), size)


def dot_nt(left, right):
    return lax.dot_general(
        left, right, (((1,), (1,)), ((), ())), preferred_element_type=F32
    )


def dot_nn(left, right):
    return lax.dot_general(
        left, right, (((1,), (0,)), ((), ())), preferred_element_type=F32
    )


def kernel(
    x_in, dy_in, wu_in, wd_in, ig_out, up_out, down_out, sq_out,
    wu, ws, xy, ww, wt, wsib, hid, gact, act_t, pre, pre_t, pre_sib,
    part, r1r, r1l, r2r, r2l, red, land,
    py, y1r, y1l, y2r, y2l, ty, z_r, z_l, fz, ox, up_t, squares, nb,
    send, recv, local,
):
    dp, mp = lax.axis_index("dp"), lax.axis_index("mp")
    z, xh = lax.div(dp, 2), lax.rem(dp, 2)
    y, xl, c = lax.div(mp, 4), lax.rem(lax.div(mp, 2), 2), lax.rem(mp, 2)
    x = 2 * xh + xl

    def device(px, py_, pz, pc):
        return (pz * 2 + lax.div(px, 2), py_ * 4 + lax.rem(px, 2) * 2 + pc)

    def at_x(k):
        return device(step(x, k, NX), y, z, c)

    def at_y(k):
        return device(x, step(y, k, NY), z, c)

    def at_z(k):
        return device(x, y, step(z, k, NZ), c)

    sibling = device(x, y, z, 1 - c)

    started = []

    def push(src, dst, target):
        n = len(started)
        copy = pltpu.make_async_remote_copy(
            src_ref=src, dst_ref=dst, send_sem=send.at[n], recv_sem=recv.at[n],
            device_id=target, device_id_type=MESH,
        )
        copy.start()
        started.append(copy)
        return copy

    moved = []

    def move(src, dst):
        copy = pltpu.make_async_copy(src, dst, local.at[len(moved)])
        copy.start()
        moved.append(copy)
        return copy

    def land_all(copies):
        for copy in copies:
            copy.wait_recv()

    wu_own = move(wu_in, wu)
    wd_own = move(wd_in, ws.at[1])

    barrier = pltpu.get_barrier_semaphore()
    plane = [
        device(step(x, i, NX), step(y, j, NY), z, c)
        for i in range(NX) for j in range(NY) if i or j
    ]
    column = [
        device(x, y, step(z, k, NZ), pc)
        for k in range(NZ) for pc in (c, 1 - c) if k or pc is not c
    ]
    peers = (
        [at_x(k) for k in range(1, NX)]
        + [at_y(k) for k in range(1, NY)]
        + [at_z(k) for k in range(1, NZ)]
        + [sibling]
    )
    for peer in peers:
        pl.semaphore_signal(barrier, inc=1, device_id=peer, device_id_type=MESH)

    pl.semaphore_wait(barrier, len(peers))

    first, rest = pl.ds(0, CUT), pl.ds(CUT, 4 * KB - CUT)

    def rows(pz):
        return span(pz * TZ, TZ)

    def half(pz, which):
        return span(pz * TZ + which * XT, XT)

    def cols(pz):
        return span(pz * KB, KB)

    def tok_place(a):
        return xy.at[c, y, span(z * TZ + xh * XT, XT), span((xl * 2 + a) * KB, KB)]

    tok, tok_own = [], []
    for k in (1, 3, 2):
        px = step(x, k, NX)
        for a, source in ((0, x_in), (1, dy_in)):
            tok.append(push(source.at[span(px * XT, XT), :], tok_place(a), at_x(k)))
    for a, source in ((0, x_in), (1, dy_in)):
        tok_own.append(move(source.at[span(x * XT, XT), :], tok_place(a)))

    wu_own.wait()

    @pl.loop(0, NZ)
    def _(t):
        at = span(t * UB, UB)
        ws[0, at, :] = wu[:, at].T

    wd_own.wait()
    w_place = ww.at[x, :, :, cols(z)]
    wz = {}

    def w_send(k):
        wz[k] = push(ws.at[:, span(step(z, k, NZ) * UB, UB), :], w_place, at_z(k))

    w_send(1)
    w_send(7)
    w_own = move(ws.at[:, span(z * UB, UB), :], w_place)

    wx1, wx2 = {}, {}

    direct = (3, 5, 4)

    def w_hop1(k):
        if k:
            wz[k].wait_recv()
        piece = ww.at[x, :, :, cols(step(z, -k, NZ))]
        wx1[k] = [push(piece, piece, at_x(1)), push(piece, piece, at_x(-1))]
        if k in direct:
            wx2[k] = [push(piece, piece, at_x(2))]

    def w_hop2(k):
        land_all(wx1[k])
        if k in direct:
            return
        pz = cols(step(z, -k, NZ))
        right = ww.at[step(x, -1, NX), 0, :, pz]
        left = ww.at[step(x, 1, NX), 1, :, pz]
        wx2[k] = [push(right, right, at_x(1)), push(left, left, at_x(-1))]

    ya1, ya2, ca, cb, za, zb = {}, {}, {}, {}, {}, {}

    def ya_hop1(k):
        block = xy.at[c, y, rows(step(z, k, NZ)), first]
        ya1[k] = [push(block, block, at_y(1)), push(block, block, at_y(-1))]

    def ya_hop2(k):
        land_all(ya1[k])
        pz = step(z, k, NZ)
        right = xy.at[c, step(y, -1, NY), half(pz, 0), first]
        left = xy.at[c, step(y, 1, NY), half(pz, 1), first]
        ya2[k] = [push(right, right, at_y(1)), push(left, left, at_y(-1))]

    def ya_core(k):
        land_all(ya2[k])
        block = xy.at[c, :, rows(step(z, k, NZ)), first]
        ca[k] = push(block, block, sibling)

    def za_step(k):
        if k < 4:
            right = xy.at[c, y, rows(step(z, 1 - k, NZ)), first]
            left = xy.at[c, y, rows(step(z, k - 1, NZ)), first]
        else:
            right = xy.at[c, y, half(step(z, 1 - k, NZ), 0), first]
            left = xy.at[c, y, half(step(z, k - 1, NZ), 1), first]
        za[k] = [push(right, right, at_z(1)), push(left, left, at_z(-1))]

    def zb_step(k):
        if k < 4:
            right = xy.at[c, :, rows(step(z, 1 - k, NZ)), rest]
            left = xy.at[c, :, rows(step(z, k - 1, NZ)), rest]
        else:
            right = xy.at[c, :, half(step(z, 1 - k, NZ), 0), rest]
            left = xy.at[c, :, half(step(z, k - 1, NZ), 1), rest]
        zb[k] = [push(right, right, at_z(1)), push(left, left, at_z(-1))]

    def cb_core(k):
        block = xy.at[c, :, rows(step(z, k, NZ)), rest]
        cb[k] = push(block, block, sibling)

    def weight(which, pc, start):
        return ww[pl.ds(2 * pc, 2), which, :, span(start, KB)].reshape(UN, KB)

    def turn(k):
        land_all(wx2[k])
        pz = step(z, -k, NZ)

        @pl.loop(0, 2, unroll=2)
        def _(pc):
            for a in range(2):
                wt[a, pc, pz] = weight(a, pc, pz * KB).T

    pre_far = {}

    def land_blocks(ks):
        for k in ks:
            ca[k].wait_recv()
            cb[k].wait_recv()

    late = lax.div(step(z, 4, NZ), 2)

    def hidden_sums(ks, chunks):
        places = [rows(step(z, k, NZ)) for k in ks]
        size = TZ * len(ks)

        def operand(a, pc, py_):
            got = [
                jnp.concatenate(
                    [
                        xy[pc, py_, at, pl.ds((2 * n + a) * KB, KB)]
                        for n in range(2)
                    ],
                    axis=1,
                )
                for at in places
            ]
            return got[0] if len(got) == 1 else jnp.concatenate(got, axis=0)

        if chunks[0] == 1:
            hid[:size] = jnp.zeros((size, UN), F32)
            gact[:size] = jnp.zeros((size, UN), F32)

        @pl.loop(0, 2 * len(chunks), unroll=2 * len(chunks))
        def _(p):
            pc = lax.rem(p, 2)
            py_ = lax.rem(late + chunks[0] + lax.div(p, 2), NY)
            for a, total in ((0, hid), (1, gact)):
                right = wt[a, pc, pl.ds(2 * py_, 2)].reshape(2 * KB, UN)
                total[:size] += dot_nn(operand(a, pc, py_), right)

    def hidden_ends(ks):
        places = [rows(step(z, k, NZ)) for k in ks]
        for n, (k, at) in enumerate(zip(ks, places)):
            pz = step(z, k, NZ)
            h = hid[n * TZ : (n + 1) * TZ]
            both = 0.5 * (1.0 + lax.erf(h * root_half))
            act = (h * both).astype(BF)
            slope = both + h * jnp.exp(-0.5 * h * h) * inv_root_two_pi
            grad = (gact[n * TZ : (n + 1) * TZ] * slope).astype(BF)
            pre[pz] = grad
            pre_t[:, at] = grad.T
            act_t[:, at] = act.T
            pre_far[k] = push(pre.at[pz], pre_sib.at[pz], sibling)

    for copy in tok_own:
        copy.wait()
    land_all(tok)
    block = xy.at[c, y, rows(z), rest]
    yb1 = [push(block, block, at_y(1)), push(block, block, at_y(-1))]
    za_step(1)
    ya_hop1(0)
    w_send(2)
    w_send(6)
    w_own.wait()
    w_hop1(0)
    w_hop1(1)
    w_hop1(7)

    land_all(yb1)
    right = xy.at[c, step(y, -1, NY), half(z, 0), rest]
    left = xy.at[c, step(y, 1, NY), half(z, 1), rest]
    yb2 = [push(right, right, at_y(1)), push(left, left, at_y(-1))]
    land_all(za[1])
    za_step(2)
    ya_hop1(1)
    ya_hop1(-1)
    ya_hop2(0)
    land_all(yb2)
    zb_step(1)
    cb_core(0)
    w_hop1(2)
    w_hop1(6)
    w_hop2(0)
    w_hop2(1)
    w_hop2(7)
    land_all(za[2])
    za_step(3)
    ya_hop1(2)
    ya_hop1(-2)
    w_send(3)
    w_send(5)
    ya_hop2(1)
    ya_hop2(-1)
    ya_core(0)
    land_all(zb[1])
    zb_step(2)
    cb_core(1)
    cb_core(-1)
    w_hop2(2)
    w_hop2(6)
    turn(0)
    turn(1)
    turn(7)
    land_all(za[3])
    za_step(4)
    w_send(4)
    ya_hop1(3)
    ya_hop1(-3)
    turn(2)
    turn(6)
    ya_hop2(2)
    ya_hop2(-2)
    ya_core(1)
    ya_core(-1)
    w_hop1(3)
    w_hop1(5)
    land_all(zb[2])
    zb_step(3)
    cb_core(2)
    cb_core(-2)
    land_all(za[4])
    ya_hop1(4)
    ya_hop2(3)
    ya_hop2(-3)
    ya_core(2)
    ya_core(-2)
    w_hop2(3)
    w_hop2(5)
    turn(3)
    turn(5)
    w_hop1(4)
    early = (0, 1, -1, 2, -2)
    land_all(zb[3])
    zb_step(4)
    cb_core(3)
    cb_core(-3)
    ya_hop2(4)
    ya_core(3)
    ya_core(-3)
    land_blocks(early)
    hidden_sums(early, (1, 2, 3))
    w_hop2(4)
    turn(4)
    w_far = push(ww.at[pl.ds(2 * (1 - c), 2), 0, :, :], wsib, sibling)
    ya_core(4)
    hidden_sums(early, (4,))
    hidden_ends(early)
    land_all(zb[4])
    cb_core(4)
    land_blocks((3, -3, 4))
    hidden_sums((3, -3, 4), (1, 2, 3, 4))
    hidden_ends((3, -3, 4))

    def grad_parts(pc, a):
        left = pre_t if a == 0 else act_t

        @pl.loop(0, NZ, unroll=4)
        def _(q):
            right = xy[
                pc, lax.div(q, 2), :, span((2 * lax.rem(q, 2) + a) * KB, KB)
            ]
            out = dot_nn(left[...], right).astype(BF)
            part[2 * pc, a, :, cols(q)] = out[:UB]
            part[2 * pc + 1, a, :, cols(q)] = out[UB:]

    far, nxt, prv = step(x, 2, NX), step(x, 1, NX), step(x, -1, NX)
    x1, x2, gz, gz_own = {}, {}, {}, {}

    def piece(q):
        return pl.ds(PIECES[q], PIECES[q + 1] - PIECES[q])

    def x_step1(q, a):
        src = part.at[far, a, piece(q), :]
        if a == 0:
            x1[q] = [push(src, r1r.at[piece(q), :], at_x(1))]
        else:
            x1[q].append(push(src, r1l.at[piece(q), :], at_x(-1)))

    def x_step2(q):
        land_all(x1[q])
        at = piece(q)
        for px, a, got in ((nxt, 0, r1r), (prv, 1, r1l)):
            total = part[px, a, at, :].astype(F32) + got[at, :].astype(F32)
            part[px, a, at, :] = total.astype(BF)
        x2[q] = [
            push(part.at[nxt, :, at, :], r2r.at[:, at, :], at_x(1)),
            push(part.at[prv, :, at, :], r2l.at[:, at, :], at_x(-1)),
        ]

    def x_sum(q):
        land_all(x2[q])
        at = piece(q)
        for a in range(2):
            total = (
                part[x, a, at, :].astype(F32)
                + r2r[a, at, :].astype(F32)
                + r2l[a, at, :].astype(F32)
            ).astype(BF)
            red[a, at, :] = total
            v = total.astype(F32)
            squares[...] += jnp.sum(v * v, axis=0, keepdims=True)

    def x_spread(q):
        at = piece(q)
        place = land.at[:, pl.ds(pl.multiple_of(z * UB + PIECES[q], 16), at.size), :]
        gz[q] = [
            push(red.at[:, at, cols(step(z, k, NZ))], place, at_z(k))
            for k in (1, 7, 2, 6, 3, 5, 4)
        ]
        gz_own[q] = move(red.at[:, at, cols(z)], place)

    def x_step3(q):
        x_sum(q)
        x_spread(q)

    pieces = (2, 1, 3, 0)
    size = NZ * XT

    def ig_own(py_, j):
        px = step(x, pieces[j], NX)
        tokens = span(lax.div(px, 2) * XT, XT)
        start = (2 * py_ + lax.rem(px, 2)) * KB
        near = weight(0, c, start)
        other = wsib[:, :, span(start, KB)].reshape(UN, KB)
        return dot_nn(pre[:, tokens, :].reshape(size, UN), near) + dot_nn(
            pre_sib[:, tokens, :].reshape(size, UN), other
        )

    y1, y2 = {}, {}
    low, high = pl.ds(0, size // 2), pl.ds(size // 2, size // 2)

    def y_step1(j):
        py[0, j] = ig_own(step(y, 2, NY), j).astype(BF)
        y1[j] = [
            push(py.at[0, j, low, :], y1r.at[j], at_y(1)),
            push(py.at[0, j, high, :], y1l.at[j], at_y(-1)),
        ]

    def y_step2(j):
        total = ig_own(step(y, 1, NY), j)
        y1[j][0].wait_recv()
        py[1, j, low, :] = (total[: size // 2] + y1r[j].astype(F32)).astype(BF)
        py[1, j, high, :] = total[size // 2 :].astype(BF)
        right = push(py.at[1, j], y2r.at[j], at_y(1))
        total = ig_own(step(y, -1, NY), j)
        y1[j][1].wait_recv()
        py[2, j, low, :] = total[: size // 2].astype(BF)
        py[2, j, high, :] = (total[size // 2 :] + y1l[j].astype(F32)).astype(BF)
        y2[j] = [right, push(py.at[2, j], y2l.at[j], at_y(-1))]

    def y_step3(j):
        total = ig_own(y, j)
        land_all(y2[j])
        ty[j] = (total + y2r[j].astype(F32) + y2l[j].astype(F32)).astype(BF)

    iz = {}
    XH = XT // 2

    def band(pz):
        return span(pz * XT, XT)

    def part_band(pz, which):
        return span(pz * XT + which * XH, XH)

    def z_step(j, k):
        right, left = step(z, 5 - k, NZ), step(z, k - 5, NZ)
        if k == 1:
            iz[j, 1] = [
                push(ty.at[j, part_band(right, 0), :], z_r.at[j, 0, pl.ds(0, XH), :], at_z(1)),
                push(ty.at[j, part_band(left, 1), :], z_l.at[j, 0, pl.ds(XH, XH), :], at_z(-1)),
            ]
            return
        land_all(iz[j, k - 1])
        if k == 2:
            add_r, add_l = part_band(right, 0), part_band(left, 1)
            got_r, got_l = z_r[j, 0, :XH], z_l[j, 0, XH:]
        else:
            add_r, add_l = band(right), band(left)
            got_r, got_l = z_r[j, k - 2], z_l[j, k - 2]
        for at, got in ((add_r, got_r), (add_l, got_l)):
            ty[j, at, :] = (ty[j, at, :].astype(F32) + got.astype(F32)).astype(BF)
        iz[j, k] = [
            push(ty.at[j, band(right), :], z_r.at[j, k - 1], at_z(1)),
            push(ty.at[j, band(left), :], z_l.at[j, k - 1], at_z(-1)),
        ]

    far_out = []

    def z_last(j):
        land_all(iz[j, 4])
        total = (
            ty[j, band(z), :].astype(F32)
            + z_r[j, 3].astype(F32)
            + z_l[j, 3].astype(F32)
        ).astype(BF)
        if pieces[j]:
            fz[j] = total
            far_out.append(
                push(fz.at[j], ox.at[span(x * XT, XT), :], at_x(pieces[j]))
            )
        else:
            ox[span(x * XT, XT), :] = total

    squares[...] = jnp.zeros_like(squares)
    grad_parts(1 - xh, 0)
    for q in range(4):
        x_step1(q, 0)
    for k in pre_far:
        pre_far[k].wait_recv()
    w_far.wait_recv()
    y_step1(0)
    y_step1(1)
    grad_parts(1 - xh, 1)
    for q in range(4):
        x_step1(q, 1)
    y_step1(2)
    grad_parts(xh, 0)
    grad_parts(xh, 1)
    x_step2(0)
    x_step2(1)
    y_step2(0)
    x_step2(2)
    y_step1(3)
    y_step2(1)
    for q in (4, 5):
        x_step1(q, 0)
        x_step1(q, 1)
    x_step3(0)
    y_step2(2)
    x_step3(1)
    y_step3(0)
    z_step(0, 1)
    x_step2(3)
    y_step2(3)
    x_step3(2)
    y_step3(1)
    z_step(1, 1)
    z_step(0, 2)
    x_step2(4)
    x_step2(5)
    y_step3(2)
    z_step(2, 1)
    z_step(1, 2)
    z_step(0, 3)
    x_step3(3)
    z_step(2, 2)
    y_step3(3)
    z_step(3, 1)
    x_sum(4)
    x_sum(5)

    value = jnp.sum(squares[...], axis=1, keepdims=True)

    def exchange(stage, me, targets, value):
        nb[stage, me] = jnp.broadcast_to(value, (8, 128))
        return [push(nb.at[stage, me], nb.at[stage, me], t) for t in targets]

    def collect(stage, copies):
        land_all(copies)
        total = nb[stage, 0]
        for n in range(1, 16):
            total = total + nb[stage, n]
        return total[:1, :1]

    norm = exchange(0, 2 * z + c, column, value)
    z_step(1, 3)
    z_step(2, 3)
    x_spread(4)
    x_spread(5)
    z_step(3, 2)
    z_step(0, 4)
    z_step(1, 4)
    z_step(2, 4)
    value = collect(0, norm)
    norm = exchange(1, 4 * x + y, plane, value)
    z_step(3, 3)
    z_last(0)
    z_last(1)
    z_last(2)
    z_step(3, 4)
    for q in gz:
        gz_own[q].wait()
        land_all(gz[q])
    down_copy = move(land.at[1], down_out)

    @pl.loop(0, NZ)
    def _(t):
        at = span(t * UB, UB)
        up_t[:, at] = land[0, at, :].T

    up_copy = move(up_t, up_out)
    value = collect(1, norm)
    sq_out[0, 0] = jnp.max(value)
    z_last(3)
    land_all(far_out)
    ig_out[...] = ox[...]
    down_copy.wait()
    up_copy.wait()

    for copy in started:
        copy.wait_send()


def on_device(inputs, cotangent, w_up, w_down):
    vmem = pl.BlockSpec(memory_space=pltpu.VMEM)
    hbm = pl.BlockSpec(memory_space=pl.ANY)
    smem = pl.BlockSpec(memory_space=pltpu.SMEM)
    ig, up, down, total = pl.pallas_call(
        kernel,
        out_shape=(
            jax.ShapeDtypeStruct((NX * XT, KB), BF),
            jax.ShapeDtypeStruct((KB, NZ * UB), BF),
            jax.ShapeDtypeStruct((NZ * UB, KB), BF),
            jax.ShapeDtypeStruct((1, 1), F32),
        ),
        in_specs=[hbm] * 4,
        out_specs=(vmem, hbm, hbm, smem),
        scratch_shapes=[
            pltpu.VMEM((KB, NZ * UB), BF),
            pltpu.VMEM((2, NZ * UB, KB), BF),
            pltpu.VMEM((2, NY, TOK, 4 * KB), BF),
            pltpu.VMEM((NX, 2, UB, ROW), BF),
            pltpu.VMEM((2, 2, NZ, KB, UN), BF),
            pltpu.VMEM((2, UB, ROW), BF),
            pltpu.VMEM((5 * TZ, UN), F32),
            pltpu.VMEM((5 * TZ, UN), F32),
            pltpu.VMEM((UN, TOK), BF),
            pltpu.VMEM((NZ, TZ, UN), BF),
            pltpu.VMEM((UN, TOK), BF),
            pltpu.VMEM((NZ, TZ, UN), BF),
            pltpu.VMEM((NX, 2, UB, ROW), BF),
            pltpu.VMEM((UB, ROW), BF),
            pltpu.VMEM((UB, ROW), BF),
            pltpu.VMEM((2, UB, ROW), BF),
            pltpu.VMEM((2, UB, ROW), BF),
            pltpu.VMEM((2, UB, ROW), BF),
            pltpu.VMEM((2, NZ * UB, KB), BF),
            pltpu.VMEM((3, 4, NZ * XT, KB), BF),
            pltpu.VMEM((4, NZ * XT // 2, KB), BF),
            pltpu.VMEM((4, NZ * XT // 2, KB), BF),
            pltpu.VMEM((4, NZ * XT, KB), BF),
            pltpu.VMEM((4, NZ * XT, KB), BF),
            pltpu.VMEM((4, NZ * XT, KB), BF),
            pltpu.VMEM((4, 4, XT, KB), BF),
            pltpu.VMEM((4, 4, XT, KB), BF),
            pltpu.VMEM((4, XT, KB), BF),
            pltpu.VMEM((NX * XT, KB), BF),
            pltpu.VMEM((KB, NZ * UB), BF),
            pltpu.VMEM((1, ROW), F32),
            pltpu.VMEM((2, 16, 8, 128), F32),
            pltpu.SemaphoreType.DMA((304,)),
            pltpu.SemaphoreType.DMA((304,)),
            pltpu.SemaphoreType.DMA((24,)),
        ],
        compiler_params=pltpu.CompilerParams(
            collective_id=0, has_side_effects=True, vmem_limit_bytes=60 * 2**20
        ),
        cost_estimate=pl.CostEstimate(
            flops=11_000_000_000, bytes_accessed=8_000_000, transcendentals=524288
        ),
    )(inputs, cotangent, w_up, w_down)
    mean_square = total[0, 0] / jnp.float32(2.0 * D * FF)
    scale = 1.0 / jnp.sqrt(mean_square)
    return ig, up.astype(F32) * scale, down.astype(F32) * scale, mean_square


def solution(mesh):
    placed = (P("dp", "mp"), P("dp", "mp"), P("dp", "mp"), P("mp", "dp"))
    return jax.shard_map(
        on_device,
        mesh=mesh,
        in_specs=placed,
        out_specs=(P("dp", "mp"), P("dp", "mp"), P("mp", "dp"), P()),
        check_vma=False,
    )
```
